32 devices in a mesh: row: 4 (over z), col: 8 (over y, x, core).
Axes of the slice: x: 2, y: 2, z: 4, core: 2. Of those that a mesh axis runs over, the one named last changes fastest.
Arguments:
- left: float32 [2, 8192, 2560], P(None, 'row', 'col'), may hold values from -6 to 6
- right: float32 [2, 2560, 8192], P(None, 'row', 'col'), may hold values from -0.078125 to 0.078125
- prefix_owner: int32 [64], replicated, may hold values from 0 to 63, each once
- qubit_order: int32 [7], replicated, may hold values from 0 to 6, each once
Outputs:
- relaid: float32 [2, 8192, 8192], P(None, ('row', 'col'))
The draws below stay inside these ranges and needn't reach their ends.
Inputs may be any that keep to these rules, and one draw needn't show every extreme that they name: `prefix_owner`: each prefix has exactly one owner, each owner one prefix. `qubit_order`: each open qubit appears once.
All inputs are finite; a program needn't handle non-finite values.
Results may differ from the reference program's by a relative error of at most 0.00007.
Values sent between devices are 32-bit elements; how exact they have to be, the bound alone decides.
No kernel may reach another device: no remote copies, remote signals or barrier semaphores. Data moves between devices by JAX's collectives and lax.ppermute only.
A program may use at most 192 MiB of HBM per device.

```python
import jax
import jax.numpy as jnp
from jax import lax

N = 8192
LOW_BITS = 7
PREFIXES = 64
K = 2560
M = 8192


def shard_levels(own_key, shape, cuts, low, high):
    level, own = 1.0, jax.random.fold_in(own_key, 6)
    for dim, parts in cuts:
        heights = jnp.exp(jax.random.uniform(jax.random.fold_in(own, dim), (parts,), jnp.float32, low / len(cuts), high / len(cuts)))
        level = level * jnp.repeat(heights, shape[dim] // parts).reshape([-1 if axis == dim else 1 for axis in range(len(shape))])
    return level


def centred(stream_key, shape, scale, most, shards=(), held_as=jnp.bfloat16):
    factor_of = shard_levels(stream_key, shape, shards, -0.22, 0.18) if shards else 1.0
    entries = jax.random.normal(stream_key, shape, jnp.float32) * scale * factor_of
    return jnp.minimum(jnp.maximum(entries, -most), most).astype(held_as)


def setup_inputs(seed: int = 0) -> dict:
    key_of = jax.random.split(jax.random.key(seed), 5)
    left = centred(key_of[0], (2, M, K), 1.0, 6.0, ((1, 4), (2, 8)), jnp.float32)
    right = centred(key_of[1], (2, K, N), (2 * K) ** -0.5, 0.078125, ((1, 4), (2, 8)), jnp.float32)
    prefix_owner = jax.random.permutation(key_of[2], PREFIXES).astype(jnp.int32)
    qubit_order = jax.random.permutation(key_of[3], LOW_BITS).astype(jnp.int32)
    return dict(left=left, right=right, prefix_owner=prefix_owner, qubit_order=qubit_order)


def source_rows(prefix_owner, qubit_order, total, low_bits, prefixes):
    span = 2 ** low_bits
    index = jnp.arange(total, dtype=jnp.int32)
    owner = index // span
    offset = index % span
    labels = jnp.arange(prefixes, dtype=jnp.int32)
    match = (prefix_owner[None, :] == labels[:, None]).astype(jnp.int32)
    inverse = jnp.sum(match * labels[None, :], axis=1).astype(jnp.int32)
    prefix = jnp.take(inverse, owner, axis=0)
    bits = jnp.bitwise_and(jnp.right_shift(offset[:, None], qubit_order[None, :]), 1)
    powers = jnp.left_shift(jnp.ones((low_bits,), jnp.int32), jnp.arange(low_bits, dtype=jnp.int32))
    inner = jnp.sum(bits * powers[None, :], axis=1).astype(jnp.int32)
    return (prefix * span + inner).astype(jnp.int32)


def reference(left, right, prefix_owner, qubit_order):
    highest = lax.Precision.HIGHEST
    real_part = jnp.dot(left[0], right[0], preferred_element_type=jnp.float32, precision=highest) - jnp.dot(left[1], right[1], preferred_element_type=jnp.float32, precision=highest)
    imag_part = jnp.dot(left[0], right[1], preferred_element_type=jnp.float32, precision=highest) + jnp.dot(left[1], right[0], preferred_element_type=jnp.float32, precision=highest)
    source = source_rows(prefix_owner, qubit_order, M, LOW_BITS, PREFIXES)
    return jnp.stack([jnp.take(real_part, source, axis=0), jnp.take(imag_part, source, axis=0)], axis=0)
```

```python
import functools
import math

import jax
import jax.numpy as jnp
from jax import lax
from jax.experimental import pallas as pl
from jax.experimental.pallas import tpu as pltpu
from jax.sharding import PartitionSpec as P

LOW_BITS = 7
SPAN = 2**LOW_BITS
PREFIXES = 64
CHUNKS = 4
MIB = 2**20


def owner_inverse(prefix_owner):
    labels = jnp.arange(PREFIXES, dtype=jnp.int32)
    match = (prefix_owner[None, :] == labels[:, None]).astype(jnp.int32)
    return jnp.sum(match * labels[None, :], axis=1)


def qubit_one_hot(qubit_order):
    offset = jnp.arange(SPAN, dtype=jnp.int32)
    bits = jnp.bitwise_and(jnp.right_shift(offset[:, None], qubit_order[None, :]), 1)
    powers = jnp.left_shift(jnp.ones((LOW_BITS,), jnp.int32), jnp.arange(LOW_BITS, dtype=jnp.int32))
    inner = jnp.sum(bits * powers[None, :], axis=1)
    return (inner[:, None] == offset[None, :]).astype(jnp.bfloat16)


def prefix_kernel(inverse_ref, x_ref, o_ref):
    per = x_ref.shape[2] // SPAN

    def move(o, _):
        p = inverse_ref[o]
        to = pl.multiple_of(lax.rem(o, per) * SPAN, SPAN)
        at = pl.multiple_of(lax.rem(p, per) * SPAN, SPAN)
        o_ref[o // per, :, pl.ds(to, SPAN)] = x_ref[p // per, :, pl.ds(at, SPAN)]
        return 0

    lax.fori_loop(0, PREFIXES, move, 0)


def order_prefixes(x, inverse):
    return pl.pallas_call(
        prefix_kernel,
        out_shape=jax.ShapeDtypeStruct(x.shape, x.dtype),
        in_specs=[
            pl.BlockSpec(memory_space=pltpu.SMEM),
            pl.BlockSpec(memory_space=pltpu.VMEM),
        ],
        out_specs=pl.BlockSpec(memory_space=pltpu.VMEM),
        compiler_params=pltpu.CompilerParams(vmem_limit_bytes=24 * MIB),
        cost_estimate=pl.CostEstimate(flops=0, bytes_accessed=8 * x.size, transcendentals=0),
    )(inverse, x)


def halves(x):
    hi = x.astype(jnp.bfloat16)
    return hi, (x - hi.astype(jnp.float32)).astype(jnp.bfloat16)


def left_kernel(hot_ref, x_ref, hi_ref, lo_ref):
    slices, _, depth, _ = x_ref.shape
    turn = functools.partial(
        lax.dot_general,
        dimension_numbers=(((1,), (1,)), ((), ())),
        preferred_element_type=jnp.float32,
    )
    for part in range(2):
        hi, lo = halves(x_ref[:, part].reshape(slices * depth, SPAN))
        hi_ref[part] = turn(hot_ref[...], hi).astype(jnp.bfloat16)
        lo_ref[part] = turn(hot_ref[...], lo).astype(jnp.bfloat16)


def prepare_left(gathered, hot):
    count, _, depth, rows = gathered.shape
    slices = 128 // math.gcd(depth, 128)
    half = jax.ShapeDtypeStruct((2, rows, count * depth), jnp.bfloat16)
    out_spec = pl.BlockSpec((2, SPAN, slices * depth), lambda j, c: (0, j, c))
    return pl.pallas_call(
        left_kernel,
        grid=(rows // SPAN, count // slices),
        out_shape=(half, half),
        in_specs=[
            pl.BlockSpec((SPAN, SPAN), lambda j, c: (0, 0)),
            pl.BlockSpec((slices, 2, depth, SPAN), lambda j, c: (c, 0, 0, j)),
        ],
        out_specs=(out_spec, out_spec),
        compiler_params=pltpu.CompilerParams(vmem_limit_bytes=24 * MIB),
        cost_estimate=pl.CostEstimate(
            flops=4 * gathered.size * SPAN, bytes_accessed=8 * gathered.size, transcendentals=0
        ),
    )(hot, gathered)


def product_kernel(hi_ref, lo_ref, right_ref, o_ref, high, low):
    shards, _, depth, _ = right_ref.shape
    piece = o_ref.shape[2]

    @pl.when(pl.program_id(0) == 0)
    def _():
        for shard in range(shards):
            at = pl.ds(shard * depth, depth)
            for part in range(2):
                high[part, at], low[part, at] = halves(right_ref[shard, part])

    dot = functools.partial(jnp.dot, preferred_element_type=jnp.float32)

    def three(i, j):
        return (
            dot(hi_ref[i], high[j]) + dot(hi_ref[i], low[j]) + dot(lo_ref[i], high[j])
        )

    real = three(0, 0) - three(1, 1)
    imag = three(0, 1) + three(1, 0)
    for n in range(o_ref.shape[0]):
        o_ref[n, 0] = real[n * piece : (n + 1) * piece]
        o_ref[n, 1] = imag[n * piece : (n + 1) * piece]


def product(hi, lo, right, count):
    _, rows, total = hi.shape
    shards, _, depth, width = right.shape
    piece = rows // count
    tile = min(512, rows)
    spec = pl.BlockSpec((2, tile, total), lambda m: (0, m, 0))
    return pl.pallas_call(
        product_kernel,
        grid=(rows // tile,),
        out_shape=jax.ShapeDtypeStruct((count, 2, piece, width), jnp.float32),
        in_specs=[
            spec,
            spec,
            pl.BlockSpec((shards, 2, depth, width), lambda m: (0, 0, 0, 0)),
        ],
        out_specs=pl.BlockSpec((tile // piece, 2, piece, width), lambda m: (m, 0, 0, 0)),
        scratch_shapes=[
            pltpu.VMEM((2, total, width), jnp.bfloat16),
            pltpu.VMEM((2, total, width), jnp.bfloat16),
        ],
        compiler_params=pltpu.CompilerParams(vmem_limit_bytes=56 * MIB),
        cost_estimate=pl.CostEstimate(
            flops=24 * rows * total * width,
            bytes_accessed=8 * rows * total + 8 * total * width + 8 * rows * width,
            transcendentals=0,
        ),
    )(hi, lo, right)


def place_kernel(*refs):
    refs[-1][...] = refs[0][0]


def place(received, out, chunk, chunks):
    count, _, rows, width = received.shape
    in_specs = [pl.BlockSpec((1, 2, rows, width), lambda c: (c, 0, 0, 0))]
    operands = [received]
    if out is not None:
        in_specs.append(pl.BlockSpec(memory_space=pl.ANY))
        operands.append(out)
    return pl.pallas_call(
        place_kernel,
        grid=(count,),
        out_shape=jax.ShapeDtypeStruct((2, rows, count * chunks * width), jnp.float32),
        in_specs=in_specs,
        out_specs=pl.BlockSpec((2, rows, width), lambda c: (0, 0, c * chunks + chunk)),
        input_output_aliases={} if out is None else {1: 0},
        compiler_params=pltpu.CompilerParams(vmem_limit_bytes=16 * MIB),
        cost_estimate=pl.CostEstimate(
            flops=0, bytes_accessed=8 * received.size, transcendentals=0
        ),
    )(*operands)


def body(left, right, prefix_owner, qubit_order):
    row_count = lax.axis_size("row")
    col_count = lax.axis_size("col")
    _, rows, depth = left.shape
    cols = right.shape[2]
    width = cols // CHUNKS
    inverse = owner_inverse(prefix_owner)
    hot = qubit_one_hot(qubit_order)

    turned = jnp.transpose(left, (0, 2, 1)).reshape(row_count, 2 * depth // row_count, rows)
    spread = lax.all_to_all(turned, "row", split_axis=0, concat_axis=0, tiled=True)
    right, spread = lax.optimization_barrier((right, spread))
    ordered = order_prefixes(spread, inverse)
    landed = lax.all_to_all(ordered, "row", split_axis=0, concat_axis=0, tiled=True)
    gathered = lax.all_gather(landed.reshape(2, depth, rows), "col", axis=0)
    hi, lo = prepare_left(gathered, hot)

    out = None
    for chunk in range(CHUNKS):
        piece = right[:, :, chunk * width : (chunk + 1) * width]
        whole = lax.all_gather(piece, "row", axis=0)
        tile = product(hi, lo, whole, col_count)
        received = lax.all_to_all(tile, "col", split_axis=0, concat_axis=0, tiled=True)
        out = place(received, out, chunk, CHUNKS)
    return out


def solution(mesh):
    in_specs = (P(None, "row", "col"), P(None, "row", "col"), P(), P())
    out_specs = P(None, ("row", "col"), None)
    return jax.shard_map(body, mesh=mesh, in_specs=in_specs, out_specs=out_specs, check_vma=False)
```

```python
import functools
import math

import jax
import jax.numpy as jnp
from jax import lax
from jax.experimental import pallas as pl
from jax.experimental.pallas import tpu as pltpu
from jax.sharding import PartitionSpec as P

LOW_BITS = 7
SPAN = 2**LOW_BITS
PREFIXES = 64
CHUNKS = 4
KGROUPS = 4
MIB = 2**20


def owner_inverse(prefix_owner):
    labels = jnp.arange(PREFIXES, dtype=jnp.int32)
    match = (prefix_owner[None, :] == labels[:, None]).astype(jnp.int32)
    return jnp.sum(match * labels[None, :], axis=1)


def qubit_one_hot(qubit_order):
    offset = jnp.arange(SPAN, dtype=jnp.int32)
    bits = jnp.bitwise_and(jnp.right_shift(offset[:, None], qubit_order[None, :]), 1)
    powers = jnp.left_shift(jnp.ones((LOW_BITS,), jnp.int32), jnp.arange(LOW_BITS, dtype=jnp.int32))
    inner = jnp.sum(bits * powers[None, :], axis=1)
    return (inner[:, None] == offset[None, :]).astype(jnp.bfloat16)


def prefix_kernel(inverse_ref, x_ref, o_ref):
    per = x_ref.shape[2] // SPAN

    def move(o, _):
        p = inverse_ref[o]
        to = pl.multiple_of(lax.rem(o, per) * SPAN, SPAN)
        at = pl.multiple_of(lax.rem(p, per) * SPAN, SPAN)
        o_ref[o // per, :, pl.ds(to, SPAN)] = x_ref[p // per, :, pl.ds(at, SPAN)]
        return 0

    lax.fori_loop(0, PREFIXES, move, 0)


def order_prefixes(x, inverse):
    return pl.pallas_call(
        prefix_kernel,
        out_shape=jax.ShapeDtypeStruct(x.shape, x.dtype),
        in_specs=[
            pl.BlockSpec(memory_space=pltpu.SMEM),
            pl.BlockSpec(memory_space=pltpu.VMEM),
        ],
        out_specs=pl.BlockSpec(memory_space=pltpu.VMEM),
        compiler_params=pltpu.CompilerParams(vmem_limit_bytes=24 * MIB),
        cost_estimate=pl.CostEstimate(flops=0, bytes_accessed=8 * x.size, transcendentals=0),
    )(inverse, x)


def halves(x):
    hi = x.astype(jnp.bfloat16)
    return hi, (x - hi.astype(jnp.float32)).astype(jnp.bfloat16)


def left_kernel(pair, parts, core_ref, hot_ref, *refs):
    first = jnp.concatenate([ref[...] for ref in refs[:parts]], axis=0)
    if pair:
        other = jnp.concatenate([ref[...] for ref in refs[parts : 2 * parts]], axis=0)
        even = core_ref[0] == 0
        block = jnp.concatenate(
            [jnp.where(even, first, other), jnp.where(even, other, first)], axis=0
        )
    else:
        block = first
    hi_ref, lo_ref = refs[-2:]
    hi, lo = halves(block)
    for n in range(block.shape[1] // SPAN):
        at = slice(n * SPAN, (n + 1) * SPAN)
        for half, ref in ((hi, hi_ref), (lo, lo_ref)):
            ref[0, at] = lax.dot_general(
                hot_ref[...],
                half[:, at],
                (((1,), (1,)), ((), ())),
                preferred_element_type=jnp.float32,
            ).astype(jnp.bfloat16)


def prepare_left(halved, part, slot, total, hot, core, first, other):
    pieces = list(first) + list(other)
    rows = first[0].shape[1]
    group = total // KGROUPS
    wide = min(2 * SPAN, rows)
    half = jax.ShapeDtypeStruct((2, rows, total), jnp.bfloat16)
    if other:
        blocks = 1
        specs = [pl.BlockSpec((x.shape[0], wide), lambda j, g: (0, j)) for x in pieces]
    else:
        blocks = KGROUPS
        specs = [pl.BlockSpec((group, wide), lambda j, g: (g, j))]
    in_specs = [
        pl.BlockSpec(memory_space=pltpu.SMEM),
        pl.BlockSpec((SPAN, SPAN), lambda j, g: (0, 0)),
    ] + specs
    operands = [core, hot] + pieces
    aliases = {}
    if halved is not None:
        aliases = {len(operands): 0, len(operands) + 1: 1}
        in_specs += [pl.BlockSpec(memory_space=pl.ANY)] * 2
        operands += list(halved)

    def kernel(core_ref, hot_ref, *refs):
        refs = refs[: len(pieces)] + refs[-2:]
        left_kernel(bool(other), len(first), core_ref, hot_ref, *refs)

    out_spec = pl.BlockSpec((1, wide, group), lambda j, g: (part, j, slot + g))
    return pl.pallas_call(
        kernel,
        grid=(rows // wide, blocks),
        out_shape=(half, half),
        in_specs=in_specs,
        out_specs=(out_spec, out_spec),
        input_output_aliases=aliases,
        compiler_params=pltpu.CompilerParams(vmem_limit_bytes=24 * MIB),
        cost_estimate=pl.CostEstimate(
            flops=4 * rows * group * blocks * SPAN,
            bytes_accessed=8 * rows * group * blocks,
            transcendentals=0,
        ),
    )(*operands)


def swap(x, distance):
    count = lax.axis_size("col")
    return lax.ppermute(x, "col", [(i, i ^ distance) for i in range(count)])


def gather_left(own, halved, part, total, hot, core):
    def prepare(halved, slot, first, other):
        return prepare_left(halved, part, slot, total, hot, core, first, other)

    half = own.shape[0] // 2
    along_x = swap(own, 2)
    along_y = swap(own, 4)
    mate = swap(own, 1)
    halved = prepare(halved, 0, [own], [mate])
    corner = [swap(along_x[:half], 4), swap(along_y[half:], 2)]
    mate_x = swap(along_x, 1)
    mate_y = swap(along_y, 1)
    halved = prepare(halved, 1, [along_x], [mate_x])
    halved = prepare(halved, 2, [along_y], [mate_y])
    return prepare(halved, 3, corner, [swap(x, 1) for x in corner])


def product_kernel(order_ref, hi_ref, lo_ref, right_ref, o_ref, high, low):
    shards, _, depth, _ = right_ref.shape
    piece = o_ref.shape[2]

    @pl.when(pl.program_id(0) == 0)
    def _():
        for shard in range(shards):
            at = pl.ds(shard * depth, depth)
            for part in range(2):
                high[part, at], low[part, at] = halves(right_ref[order_ref[shard], part])

    dot = functools.partial(jnp.dot, preferred_element_type=jnp.float32)

    def three(i, j):
        return (
            dot(hi_ref[i], high[j]) + dot(hi_ref[i], low[j]) + dot(lo_ref[i], high[j])
        )

    real = three(0, 0) - three(1, 1)
    imag = three(0, 1) + three(1, 0)
    for n in range(o_ref.shape[0]):
        o_ref[n, 0] = real[n * piece : (n + 1) * piece]
        o_ref[n, 1] = imag[n * piece : (n + 1) * piece]


def product(hi, lo, right, order, count):
    _, rows, total = hi.shape
    shards, _, depth, width = right.shape
    piece = rows // count
    tile = min(512, rows)
    spec = pl.BlockSpec((2, tile, total), lambda m: (0, m, 0))
    return pl.pallas_call(
        product_kernel,
        grid=(rows // tile,),
        out_shape=jax.ShapeDtypeStruct((count, 2, piece, width), jnp.float32),
        in_specs=[
            pl.BlockSpec(memory_space=pltpu.SMEM),
            spec,
            spec,
            pl.BlockSpec((shards, 2, depth, width), lambda m: (0, 0, 0, 0)),
        ],
        out_specs=pl.BlockSpec((tile // piece, 2, piece, width), lambda m: (m, 0, 0, 0)),
        scratch_shapes=[
            pltpu.VMEM((2, total, width), jnp.bfloat16),
            pltpu.VMEM((2, total, width), jnp.bfloat16),
        ],
        compiler_params=pltpu.CompilerParams(vmem_limit_bytes=56 * MIB),
        cost_estimate=pl.CostEstimate(
            flops=24 * rows * total * width,
            bytes_accessed=8 * rows * total + 8 * total * width + 8 * rows * width,
            transcendentals=0,
        ),
    )(order, hi, lo, right)


def place_kernel(*refs):
    refs[-1][...] = refs[0][0]


def place(received, out, chunk, chunks):
    count, _, rows, width = received.shape
    in_specs = [pl.BlockSpec((1, 2, rows, width), lambda c: (c, 0, 0, 0))]
    operands = [received]
    if out is not None:
        in_specs.append(pl.BlockSpec(memory_space=pl.ANY))
        operands.append(out)
    return pl.pallas_call(
        place_kernel,
        grid=(count,),
        out_shape=jax.ShapeDtypeStruct((2, rows, count * chunks * width), jnp.float32),
        in_specs=in_specs,
        out_specs=pl.BlockSpec((2, rows, width), lambda c: (0, 0, c * chunks + chunk)),
        input_output_aliases={} if out is None else {1: 0},
        compiler_params=pltpu.CompilerParams(vmem_limit_bytes=16 * MIB),
        cost_estimate=pl.CostEstimate(
            flops=0, bytes_accessed=8 * received.size, transcendentals=0
        ),
    )(*operands)


def body(left, right, prefix_owner, qubit_order):
    row_count = lax.axis_size("row")
    col_count = lax.axis_size("col")
    _, rows, depth = left.shape
    total = depth * col_count
    cols = right.shape[2]
    width = cols // CHUNKS
    inverse = owner_inverse(prefix_owner)
    hot = qubit_one_hot(qubit_order)
    place_in_col = lax.axis_index("col")
    core = (place_in_col % 2).reshape(1)
    order = jnp.arange(row_count, dtype=jnp.int32)
    paired = col_count == 8 and row_count == 4
    if paired:
        order = order ^ (place_in_col // 2)

    turned = jnp.transpose(left, (0, 2, 1))
    halved, before = None, None
    for part in range(2):
        piece = turned[part]
        if before is not None:
            piece, before = lax.optimization_barrier((piece, before))
        piece = piece.reshape(row_count, depth // row_count, rows)
        spread = lax.all_to_all(piece, "row", split_axis=0, concat_axis=0, tiled=True)
        ordered = order_prefixes(spread, inverse)
        landed = lax.all_to_all(ordered, "row", split_axis=0, concat_axis=0, tiled=True)
        before = landed = landed.reshape(depth, rows)
        if paired:
            halved = gather_left(landed, halved, part, total, hot, core)
        else:
            gathered = lax.all_gather(landed, "col", axis=0, tiled=True)
            halved = prepare_left(halved, part, 0, total, hot, core, [gathered], [])
    hi, lo = halved
    later, spread = lax.optimization_barrier((right, spread))

    out = None
    for chunk in range(CHUNKS):
        piece = (later if chunk else right)[:, :, chunk * width : (chunk + 1) * width]
        whole = lax.all_gather(piece, "row", axis=0)
        tile = product(hi, lo, whole, order, col_count)
        received = lax.all_to_all(tile, "col", split_axis=0, concat_axis=0, tiled=True)
        out = place(received, out, chunk, CHUNKS)
    return out


def solution(mesh):
    in_specs = (P(None, "row", "col"), P(None, "row", "col"), P(), P())
    out_specs = P(None, ("row", "col"), None)
    return jax.shard_map(body, mesh=mesh, in_specs=in_specs, out_specs=out_specs, check_vma=False)
```

```python
import functools
import math

import jax
import jax.numpy as jnp
from jax import lax
from jax.experimental import pallas as pl
from jax.experimental.pallas import tpu as pltpu
from jax.sharding import PartitionSpec as P

LOW_BITS = 7
SPAN = 2**LOW_BITS
PREFIXES = 64
CHUNKS = 4
MIB = 2**20
VMEM = 58 * MIB


def owner_inverse(prefix_owner):
    labels = jnp.arange(PREFIXES, dtype=jnp.int32)
    match = (prefix_owner[None, :] == labels[:, None]).astype(jnp.int32)
    return jnp.sum(match * labels[None, :], axis=1)


def qubit_one_hot(qubit_order):
    offset = jnp.arange(SPAN, dtype=jnp.int32)
    bits = jnp.bitwise_and(jnp.right_shift(offset[:, None], qubit_order[None, :]), 1)
    powers = jnp.left_shift(jnp.ones((LOW_BITS,), jnp.int32), jnp.arange(LOW_BITS, dtype=jnp.int32))
    inner = jnp.sum(bits * powers[None, :], axis=1)
    return (inner[:, None] == offset[None, :]).astype(jnp.bfloat16)


def prefix_kernel(inverse_ref, x_ref, o_ref):
    per = x_ref.shape[2] // SPAN

    def move(o, _):
        p = inverse_ref[o]
        to = pl.multiple_of(lax.rem(o, per) * SPAN, SPAN)
        at = pl.multiple_of(lax.rem(p, per) * SPAN, SPAN)
        o_ref[o // per, :, pl.ds(to, SPAN)] = x_ref[p // per, :, pl.ds(at, SPAN)]
        return 0

    lax.fori_loop(0, PREFIXES, move, 0)


def order_prefixes(x, inverse):
    return pl.pallas_call(
        prefix_kernel,
        out_shape=jax.ShapeDtypeStruct(x.shape, x.dtype),
        in_specs=[
            pl.BlockSpec(memory_space=pltpu.SMEM),
            pl.BlockSpec(memory_space=pltpu.VMEM),
        ],
        out_specs=pl.BlockSpec(memory_space=pltpu.VMEM),
        compiler_params=pltpu.CompilerParams(vmem_limit_bytes=VMEM),
        cost_estimate=pl.CostEstimate(flops=0, bytes_accessed=8 * x.size, transcendentals=0),
    )(inverse, x)


def halves(x):
    hi = x.astype(jnp.bfloat16)
    return hi, (x - hi.astype(jnp.float32)).astype(jnp.bfloat16)


def left_kernel(hot_ref, x_ref, hi_ref, lo_ref):
    slices, _, depth, _ = x_ref.shape
    turn = functools.partial(
        lax.dot_general,
        dimension_numbers=(((1,), (1,)), ((), ())),
        preferred_element_type=jnp.float32,
    )
    for part in range(2):
        hi, lo = halves(x_ref[:, part].reshape(slices * depth, SPAN))
        hi_ref[part] = turn(hot_ref[...], hi).astype(jnp.bfloat16)
        lo_ref[part] = turn(hot_ref[...], lo).astype(jnp.bfloat16)


def prepare_left(gathered, hot):
    count, _, depth, rows = gathered.shape
    slices = 128 // math.gcd(depth, 128)
    half = jax.ShapeDtypeStruct((2, rows, count * depth), jnp.bfloat16)
    out_spec = pl.BlockSpec((2, SPAN, slices * depth), lambda j, c: (0, j, c))
    return pl.pallas_call(
        left_kernel,
        grid=(rows // SPAN, count // slices),
        out_shape=(half, half),
        in_specs=[
            pl.BlockSpec((SPAN, SPAN), lambda j, c: (0, 0)),
            pl.BlockSpec((slices, 2, depth, SPAN), lambda j, c: (c, 0, 0, j)),
        ],
        out_specs=(out_spec, out_spec),
        compiler_params=pltpu.CompilerParams(vmem_limit_bytes=VMEM),
        cost_estimate=pl.CostEstimate(
            flops=4 * gathered.size * SPAN, bytes_accessed=8 * gathered.size, transcendentals=0
        ),
    )(hot, gathered)


def exchange_kernel(owner_ref, planes_ref, slots_ref, *refs):
    sources, targets, held = refs[:4], refs[4:8], refs[8]
    per = sources[0].shape[1] // SPAN
    for s in range(4):
        for i in range(per):
            o = owner_ref[planes_ref[s] * per + i]
            to = pl.multiple_of(lax.rem(o, per) * SPAN, SPAN)
            held[slots_ref[o // per], :, pl.ds(to, SPAN)] = sources[s][:, i * SPAN : (i + 1) * SPAN]
    for s in range(4):
        targets[s][...] = held[s]


def exchange_prefixes(sources, prefix_owner, planes, slots):
    x = sources[0]
    vmem = pl.BlockSpec(memory_space=pltpu.VMEM)
    smem = pl.BlockSpec(memory_space=pltpu.SMEM)
    return pl.pallas_call(
        exchange_kernel,
        out_shape=[jax.ShapeDtypeStruct(x.shape, x.dtype)] * 4,
        in_specs=[smem] * 3 + [vmem] * 4,
        out_specs=[vmem] * 4,
        scratch_shapes=[pltpu.VMEM((4,) + x.shape, x.dtype)],
        compiler_params=pltpu.CompilerParams(vmem_limit_bytes=VMEM),
        cost_estimate=pl.CostEstimate(flops=0, bytes_accessed=32 * x.size, transcendentals=0),
    )(prefix_owner, planes, slots, *sources)


def slots_kernel(counts, core_ref, hot_ref, *refs):
    hi_ref, lo_ref = refs[-2:]
    even = core_ref[0] == 0
    for part in range(2):
        pieces = []
        at = 0
        for count in counts:
            if count == 1:
                mine, mate = refs[at][part], refs[at + 1][part]
            else:
                mine, mate = refs[at + part][...], refs[at + 2 + part][...]
            at += 2 * count
            pieces += [jnp.where(even, mine, mate), jnp.where(even, mate, mine)]
        hi, lo = halves(jnp.concatenate(pieces, axis=0))
        for n in range(hi.shape[1] // SPAN):
            span = slice(n * SPAN, (n + 1) * SPAN)
            for half, ref in ((hi, hi_ref), (lo, lo_ref)):
                ref[part, span] = lax.dot_general(
                    hot_ref[...],
                    half[:, span],
                    (((1,), (1,)), ((), ())),
                    preferred_element_type=jnp.float32,
                ).astype(jnp.bfloat16)


def prepare_slots(halved, block, blocks, hot, core, slots):
    counts, pieces = [], []
    for mine, mate in slots:
        counts.append(len(mine))
        pieces += list(mine) + list(mate)
    rows = pieces[0].shape[-1]
    wide = 2 * SPAN
    group = sum(2 * mine[0].shape[-2] for mine, _ in slots)
    half = jax.ShapeDtypeStruct((2, rows, blocks * group), jnp.bfloat16)
    in_specs = [pl.BlockSpec(memory_space=pltpu.SMEM), pl.BlockSpec((SPAN, SPAN), lambda j: (0, 0))]
    for x in pieces:
        if x.ndim == 3:
            in_specs.append(pl.BlockSpec(x.shape[:2] + (wide,), lambda j: (0, 0, j)))
        else:
            in_specs.append(pl.BlockSpec((x.shape[0], wide), lambda j: (0, j)))
    operands = [core, hot] + pieces
    aliases = {}
    if halved is not None:
        aliases = {len(operands): 0, len(operands) + 1: 1}
        in_specs += [pl.BlockSpec(memory_space=pl.ANY)] * 2
        operands += list(halved)
    out_spec = pl.BlockSpec((2, wide, group), lambda j: (0, j, block))
    return pl.pallas_call(
        functools.partial(slots_kernel, counts),
        grid=(rows // wide,),
        out_shape=(half, half),
        in_specs=in_specs,
        out_specs=(out_spec, out_spec),
        input_output_aliases=aliases,
        compiler_params=pltpu.CompilerParams(vmem_limit_bytes=VMEM),
        cost_estimate=pl.CostEstimate(
            flops=8 * rows * group * SPAN, bytes_accessed=16 * rows * group, transcendentals=0
        ),
    )(*operands)


def swap(x, distance):
    count = lax.axis_size("col")
    return lax.ppermute(x, "col", [(i, i ^ distance) for i in range(count)])


def gather_left(own, halved, half, hot, core):
    along_x = swap(own, 2)
    along_y = swap(own, 4)
    mate = swap(own, 1)
    corner = [swap(along_x[0], 4), swap(along_y[1], 2)]
    mate_x = swap(along_x, 1)
    mate_y = swap(along_y, 1)
    halved = prepare_slots(
        halved, 2 * half, 4, hot, core, [([own], [mate]), ([along_x], [mate_x])]
    )
    mate_corner = [swap(x, 1) for x in corner]
    return prepare_slots(
        halved, 2 * half + 1, 4, hot, core, [([along_y], [mate_y]), (corner, mate_corner)]
    )


def fill_whole(right_ref, high, low):
    shards, _, depth, _ = right_ref.shape
    for shard in range(shards):
        at = pl.ds(shard * depth, depth)
        for part in range(2):
            high[part, at], low[part, at] = halves(right_ref[shard, part])


def fill_shards(slot_ref, own_ref, from_inner, from_end, across, forwarded, high, low):
    depth = own_ref.shape[1]
    short = depth // 4

    def fill(slot, source):
        for part in range(2):
            for core in range(2):
                for half in range(2):
                    at = pl.multiple_of(half * 4 * depth // 2 + slot * depth // 2 + core * short, 32)
                    to = pl.ds(at, short)
                    k = core * 2 * short + half * short
                    high[part, to], low[part, to] = halves(source(part)[k : k + short])

    fill(slot_ref[1], lambda part: own_ref[part])

    @pl.when(slot_ref[0] == 1)
    def _():
        fill(slot_ref[2], lambda part: from_end[part])
        for n in range(2):
            fill(slot_ref[3 + n], lambda part, n=n: across[n, part])

    @pl.when(slot_ref[0] == 0)
    def _():
        fill(slot_ref[2], lambda part: from_inner[part])
        for n in range(2):
            fill(slot_ref[3 + n], lambda part, n=n: forwarded[n, part])


def product_kernel(fill, hi_ref, lo_ref, *refs):
    right_refs = refs[:-3]
    o_ref, high, low = refs[-3:]
    piece = o_ref.shape[2]

    @pl.when(pl.program_id(0) == 0)
    def _():
        fill(*right_refs, high, low)

    dot = functools.partial(jnp.dot, preferred_element_type=jnp.float32)

    def three(i, j):
        return (
            dot(hi_ref[i], high[j]) + dot(hi_ref[i], low[j]) + dot(lo_ref[i], high[j])
        )

    real = three(0, 0) - three(1, 1)
    imag = three(0, 1) + three(1, 0)
    for n in range(o_ref.shape[0]):
        o_ref[n, 0] = real[n * piece : (n + 1) * piece]
        o_ref[n, 1] = imag[n * piece : (n + 1) * piece]


def product(hi, lo, fill, rights, specs, count, width):
    _, rows, total = hi.shape
    piece = rows // count
    tile = min(512, rows)
    spec = pl.BlockSpec((2, tile, total), lambda m: (0, m, 0))
    return pl.pallas_call(
        functools.partial(product_kernel, fill),
        grid=(rows // tile,),
        out_shape=jax.ShapeDtypeStruct((count, 2, piece, width), jnp.float32),
        in_specs=[spec, spec] + specs,
        out_specs=pl.BlockSpec((tile // piece, 2, piece, width), lambda m: (m, 0, 0, 0)),
        scratch_shapes=[
            pltpu.VMEM((2, total, width), jnp.bfloat16),
            pltpu.VMEM((2, total, width), jnp.bfloat16),
        ],
        compiler_params=pltpu.CompilerParams(vmem_limit_bytes=VMEM),
        cost_estimate=pl.CostEstimate(
            flops=24 * rows * total * width,
            bytes_accessed=8 * rows * total + 16 * total * width + 8 * rows * width,
            transcendentals=0,
        ),
    )(hi, lo, *rights)


def place_kernel(*refs):
    refs[-1][...] = refs[0][0]


def place(received, out, chunk, chunks):
    count, _, rows, width = received.shape
    in_specs = [pl.BlockSpec((1, 2, rows, width), lambda c: (c, 0, 0, 0))]
    operands = [received]
    if out is not None:
        in_specs.append(pl.BlockSpec(memory_space=pl.ANY))
        operands.append(out)
    return pl.pallas_call(
        place_kernel,
        grid=(count,),
        out_shape=jax.ShapeDtypeStruct((2, rows, count * chunks * width), jnp.float32),
        in_specs=in_specs,
        out_specs=pl.BlockSpec((2, rows, width), lambda c: (0, 0, c * chunks + chunk)),
        input_output_aliases={} if out is None else {1: 0},
        compiler_params=pltpu.CompilerParams(vmem_limit_bytes=VMEM),
        cost_estimate=pl.CostEstimate(
            flops=0, bytes_accessed=8 * received.size, transcendentals=0
        ),
    )(*operands)


def after(x, *others):
    return lax.optimization_barrier((x,) + others)[0]


def line_body(left, right, prefix_owner, qubit_order):
    z = lax.axis_index("row")
    me = lax.axis_index("col")
    count = lax.axis_size("col")
    _, rows, depth = left.shape
    _, deep, cols = right.shape
    width = cols // CHUNKS
    hot = qubit_one_hot(qubit_order)
    core = (me % 2).reshape(1)
    chip = me // 2
    upper = (z >= 2).astype(jnp.int32)
    inner = jnp.logical_or(z == 1, z == 2)
    planes = jnp.stack([z, z ^ 1, 3 - z, (3 - z) ^ 1]).astype(jnp.int32)
    labels = jnp.arange(4, dtype=jnp.int32)
    slots = jnp.sum((planes[None, :] == labels[:, None]).astype(jnp.int32) * labels[None, :], axis=1)
    shards = jnp.stack([z, z ^ 1, 2 - upper, 3 - 3 * upper])
    table = jnp.concatenate([inner.astype(jnp.int32).reshape(1), chip ^ shards]).astype(jnp.int32)

    def along(x, pairs):
        return lax.ppermute(x, "row", pairs)

    turned = jnp.transpose(left, (0, 2, 1))
    halved, from_inner, from_end, landed = None, [], [], None
    for half in range(2):
        short, columns = depth // 2, cols // 2
        near = right[:, :, half * columns : (half + 1) * columns]
        if landed is not None:
            turned = after(turned, landed)
            near = after(near, landed)
        piece = turned[:, half * short : (half + 1) * short]
        mine = lax.dynamic_index_in_dim(piece, upper, 0, keepdims=False)
        theirs = lax.dynamic_index_in_dim(piece, 1 - upper, 0, keepdims=False)
        sources = [
            mine,
            along(mine, [(0, 1), (3, 2)]),
            along(theirs, [(1, 2), (2, 1)]),
            along(theirs, [(0, 2), (3, 1)]),
        ]
        from_inner.append(along(near, [(1, 0), (2, 3)]))
        kept, *sent = exchange_prefixes(sources, prefix_owner, planes, slots)
        near = after(near, kept)
        got = [
            along(sent[0], [(1, 0), (2, 3)]),
            along(sent[1], [(1, 2), (2, 1)]),
            along(sent[2], [(1, 3), (2, 0)]),
        ]
        from_end.append(along(near, [(0, 1), (3, 2)]))
        real = lax.select_n(z, got[0], kept, got[1], got[2])
        imag = lax.select_n(z, got[2], got[1], kept, got[0])
        landed = jnp.stack([real, imag])
        halved = gather_left(landed, halved, half, hot, core)
    hi, lo = halved

    out, before = None, landed
    for chunk in range(CHUNKS):
        half, part = divmod(chunk, CHUNKS // 2)
        pair = jnp.stack(
            [
                right[:, :, chunk * width : (chunk + 1) * width],
                from_end[half][:, :, part * width : (part + 1) * width],
            ]
        )
        across = along(after(pair, before), [(1, 2), (2, 1)])
        forwarded = along(across, [(1, 0), (2, 3)])
        before = across
        whole = pl.BlockSpec((2, 2, deep, width), lambda m: (0, 0, 0, 0))

        def columns_at(n):
            return pl.BlockSpec((2, deep, width), lambda m: (0, 0, n))

        tile = product(
            hi,
            lo,
            fill_shards,
            [table, right, from_inner[half], from_end[half], across, forwarded],
            [
                pl.BlockSpec(memory_space=pltpu.SMEM),
                columns_at(chunk),
                columns_at(part),
                columns_at(part),
                whole,
                whole,
            ],
            count,
            width,
        )
        received = lax.all_to_all(tile, "col", split_axis=0, concat_axis=0, tiled=True)
        out = place(received, out, chunk, CHUNKS)
    return out


def any_body(left, right, prefix_owner, qubit_order):
    row_count = lax.axis_size("row")
    col_count = lax.axis_size("col")
    _, rows, depth = left.shape
    _, deep, cols = right.shape
    width = cols // CHUNKS
    inverse = owner_inverse(prefix_owner)
    hot = qubit_one_hot(qubit_order)

    turned = jnp.transpose(left, (0, 2, 1)).reshape(row_count, 2 * depth // row_count, rows)
    spread = lax.all_to_all(turned, "row", split_axis=0, concat_axis=0, tiled=True)
    ordered = order_prefixes(spread, inverse)
    landed = lax.all_to_all(ordered, "row", split_axis=0, concat_axis=0, tiled=True)
    gathered = lax.all_gather(landed.reshape(2, depth, rows), "col", axis=0)
    hi, lo = prepare_left(gathered, hot)

    out = None
    for chunk in range(CHUNKS):
        piece = right[:, :, chunk * width : (chunk + 1) * width]
        whole = lax.all_gather(piece, "row", axis=0)
        spec = pl.BlockSpec((row_count, 2, deep, width), lambda m: (0, 0, 0, 0))
        tile = product(hi, lo, fill_whole, [whole], [spec], col_count, width)
        received = lax.all_to_all(tile, "col", split_axis=0, concat_axis=0, tiled=True)
        out = place(received, out, chunk, CHUNKS)
    return out


def solution(mesh):
    in_specs = (P(None, "row", "col"), P(None, "row", "col"), P(), P())
    out_specs = P(None, ("row", "col"), None)
    line = mesh.shape["row"] == 4 and mesh.shape["col"] == 8
    body = line_body if line else any_body
    return jax.shard_map(body, mesh=mesh, in_specs=in_specs, out_specs=out_specs, check_vma=False)
```

```python
import functools
import math

import jax
import jax.numpy as jnp
from jax import lax
from jax.experimental import pallas as pl
from jax.experimental.pallas import tpu as pltpu
from jax.sharding import PartitionSpec as P

LOW_BITS = 7
SPAN = 2**LOW_BITS
PREFIXES = 64
EIGHTHS = (2, 2, 2, 1, 1)
MIB = 2**20
VMEM = 58 * MIB


def owner_inverse(prefix_owner):
    labels = jnp.arange(PREFIXES, dtype=jnp.int32)
    match = (prefix_owner[None, :] == labels[:, None]).astype(jnp.int32)
    return jnp.sum(match * labels[None, :], axis=1)


def qubit_one_hot(qubit_order):
    offset = jnp.arange(SPAN, dtype=jnp.int32)
    bits = jnp.bitwise_and(jnp.right_shift(offset[:, None], qubit_order[None, :]), 1)
    powers = jnp.left_shift(jnp.ones((LOW_BITS,), jnp.int32), jnp.arange(LOW_BITS, dtype=jnp.int32))
    inner = jnp.sum(bits * powers[None, :], axis=1)
    return (inner[:, None] == offset[None, :]).astype(jnp.bfloat16)


def prefix_kernel(inverse_ref, x_ref, o_ref):
    per = x_ref.shape[2] // SPAN

    def move(o, _):
        p = inverse_ref[o]
        to = pl.multiple_of(lax.rem(o, per) * SPAN, SPAN)
        at = pl.multiple_of(lax.rem(p, per) * SPAN, SPAN)
        o_ref[o // per, :, pl.ds(to, SPAN)] = x_ref[p // per, :, pl.ds(at, SPAN)]
        return 0

    lax.fori_loop(0, PREFIXES, move, 0)


def order_prefixes(x, inverse):
    return pl.pallas_call(
        prefix_kernel,
        out_shape=jax.ShapeDtypeStruct(x.shape, x.dtype),
        in_specs=[
            pl.BlockSpec(memory_space=pltpu.SMEM),
            pl.BlockSpec(memory_space=pltpu.VMEM),
        ],
        out_specs=pl.BlockSpec(memory_space=pltpu.VMEM),
        compiler_params=pltpu.CompilerParams(vmem_limit_bytes=VMEM),
        cost_estimate=pl.CostEstimate(flops=0, bytes_accessed=8 * x.size, transcendentals=0),
    )(inverse, x)


def halves(x):
    hi = x.astype(jnp.bfloat16)
    return hi, (x - hi.astype(jnp.float32)).astype(jnp.bfloat16)


def left_kernel(hot_ref, x_ref, hi_ref, lo_ref):
    slices, _, depth, _ = x_ref.shape
    turn = functools.partial(
        lax.dot_general,
        dimension_numbers=(((1,), (1,)), ((), ())),
        preferred_element_type=jnp.float32,
    )
    for part in range(2):
        hi, lo = halves(x_ref[:, part].reshape(slices * depth, SPAN))
        hi_ref[part] = turn(hot_ref[...], hi).astype(jnp.bfloat16)
        lo_ref[part] = turn(hot_ref[...], lo).astype(jnp.bfloat16)


def prepare_left(gathered, hot):
    count, _, depth, rows = gathered.shape
    slices = 128 // math.gcd(depth, 128)
    half = jax.ShapeDtypeStruct((2, rows, count * depth), jnp.bfloat16)
    out_spec = pl.BlockSpec((2, SPAN, slices * depth), lambda j, c: (0, j, c))
    return pl.pallas_call(
        left_kernel,
        grid=(rows // SPAN, count // slices),
        out_shape=(half, half),
        in_specs=[
            pl.BlockSpec((SPAN, SPAN), lambda j, c: (0, 0)),
            pl.BlockSpec((slices, 2, depth, SPAN), lambda j, c: (c, 0, 0, j)),
        ],
        out_specs=(out_spec, out_spec),
        compiler_params=pltpu.CompilerParams(vmem_limit_bytes=VMEM),
        cost_estimate=pl.CostEstimate(
            flops=4 * gathered.size * SPAN, bytes_accessed=8 * gathered.size, transcendentals=0
        ),
    )(hot, gathered)


def exchange_kernel(owner_ref, planes_ref, slots_ref, *refs):
    sources, targets, held = refs[:4], refs[4:8], refs[8]
    per = sources[0].shape[1] // SPAN
    for s in range(4):
        for i in range(per):
            o = owner_ref[planes_ref[s] * per + i]
            to = pl.multiple_of(lax.rem(o, per) * SPAN, SPAN)
            held[slots_ref[o // per], :, pl.ds(to, SPAN)] = sources[s][:, i * SPAN : (i + 1) * SPAN]
    for s in range(4):
        targets[s][...] = held[s]


def exchange_prefixes(sources, prefix_owner, planes, slots):
    x = sources[0]
    vmem = pl.BlockSpec(memory_space=pltpu.VMEM)
    smem = pl.BlockSpec(memory_space=pltpu.SMEM)
    return pl.pallas_call(
        exchange_kernel,
        out_shape=[jax.ShapeDtypeStruct(x.shape, x.dtype)] * 4,
        in_specs=[smem] * 3 + [vmem] * 4,
        out_specs=[vmem] * 4,
        scratch_shapes=[pltpu.VMEM((4,) + x.shape, x.dtype)],
        compiler_params=pltpu.CompilerParams(vmem_limit_bytes=VMEM),
        cost_estimate=pl.CostEstimate(flops=0, bytes_accessed=32 * x.size, transcendentals=0),
    )(prefix_owner, planes, slots, *sources)


def slots_kernel(counts, core_ref, hot_ref, *refs):
    hi_ref, lo_ref = refs[-2:]
    even = core_ref[0] == 0
    for part in range(2):
        pieces = []
        at = 0
        for count in counts:
            if count == 1:
                mine, mate = refs[at][part], refs[at + 1][part]
            else:
                mine, mate = refs[at + part][...], refs[at + 2 + part][...]
            at += 2 * count
            pieces += [jnp.where(even, mine, mate), jnp.where(even, mate, mine)]
        hi, lo = halves(jnp.concatenate(pieces, axis=0))
        for n in range(hi.shape[1] // SPAN):
            span = slice(n * SPAN, (n + 1) * SPAN)
            for half, ref in ((hi, hi_ref), (lo, lo_ref)):
                ref[part, span] = lax.dot_general(
                    hot_ref[...],
                    half[:, span],
                    (((1,), (1,)), ((), ())),
                    preferred_element_type=jnp.float32,
                ).astype(jnp.bfloat16)


def prepare_slots(halved, block, blocks, hot, core, slots):
    counts, pieces = [], []
    for mine, mate in slots:
        counts.append(len(mine))
        pieces += list(mine) + list(mate)
    rows = pieces[0].shape[-1]
    wide = 2 * SPAN
    group = sum(2 * mine[0].shape[-2] for mine, _ in slots)
    half = jax.ShapeDtypeStruct((2, rows, blocks * group), jnp.bfloat16)
    in_specs = [pl.BlockSpec(memory_space=pltpu.SMEM), pl.BlockSpec((SPAN, SPAN), lambda j: (0, 0))]
    for x in pieces:
        if x.ndim == 3:
            in_specs.append(pl.BlockSpec(x.shape[:2] + (wide,), lambda j: (0, 0, j)))
        else:
            in_specs.append(pl.BlockSpec((x.shape[0], wide), lambda j: (0, j)))
    operands = [core, hot] + pieces
    aliases = {}
    if halved is not None:
        aliases = {len(operands): 0, len(operands) + 1: 1}
        in_specs += [pl.BlockSpec(memory_space=pl.ANY)] * 2
        operands += list(halved)
    out_spec = pl.BlockSpec((2, wide, group), lambda j: (0, j, block))
    return pl.pallas_call(
        functools.partial(slots_kernel, counts),
        grid=(rows // wide,),
        out_shape=(half, half),
        in_specs=in_specs,
        out_specs=(out_spec, out_spec),
        input_output_aliases=aliases,
        compiler_params=pltpu.CompilerParams(vmem_limit_bytes=VMEM),
        cost_estimate=pl.CostEstimate(
            flops=8 * rows * group * SPAN, bytes_accessed=16 * rows * group, transcendentals=0
        ),
    )(*operands)


def swap(x, distance):
    count = lax.axis_size("col")
    return lax.ppermute(x, "col", [(i, i ^ distance) for i in range(count)])


def gather_left(own, halved, half, hot, core):
    along_x = swap(own, 2)
    along_y = swap(own, 4)
    mate = swap(own, 1)
    corner = [swap(along_x[0], 4), swap(along_y[1], 2)]
    mate_x = swap(along_x, 1)
    mate_y = swap(along_y, 1)
    halved = prepare_slots(
        halved, 2 * half, 4, hot, core, [([own], [mate]), ([along_x], [mate_x])]
    )
    *corner, _ = lax.optimization_barrier((*corner, halved))
    mate_corner = [swap(x, 1) for x in corner]
    return prepare_slots(
        halved, 2 * half + 1, 4, hot, core, [([along_y], [mate_y]), (corner, mate_corner)]
    )


def put(high, low, part, at, x):
    width = x.shape[1]
    to = slice(part * width, (part + 1) * width)
    high[at, to], low[at, to] = halves(x)


def fill_whole(right_ref, high, low):
    shards, _, depth, _ = right_ref.shape
    for shard in range(shards):
        at = pl.ds(shard * depth, depth)
        for part in range(2):
            put(high, low, part, at, right_ref[shard, part])


def fill_shards(slot_ref, own_ref, from_inner, from_end, across, forwarded, high, low):
    depth = own_ref.shape[1]
    short = depth // 4

    def fill(slot, source):
        for part in range(2):
            for core in range(2):
                for half in range(2):
                    at = pl.multiple_of(half * 4 * depth // 2 + slot * depth // 2 + core * short, 32)
                    to = pl.ds(at, short)
                    k = core * 2 * short + half * short
                    put(high, low, part, to, source(part)[k : k + short])

    fill(slot_ref[1], lambda part: own_ref[part])

    @pl.when(slot_ref[0] == 1)
    def _():
        fill(slot_ref[2], lambda part: from_end[part])
        for n in range(2):
            fill(slot_ref[3 + n], lambda part, n=n: across[n, part])

    @pl.when(slot_ref[0] == 0)
    def _():
        fill(slot_ref[2], lambda part: from_inner[part])
        for n in range(2):
            fill(slot_ref[3 + n], lambda part, n=n: forwarded[n, part])


def product_kernel(fill, hi_ref, lo_ref, *refs):
    right_refs = refs[:-3]
    o_ref, high, low = refs[-3:]
    piece = o_ref.shape[2]

    @pl.when(pl.program_id(0) == 0)
    def _():
        fill(*right_refs, high, low)

    dot = functools.partial(jnp.dot, preferred_element_type=jnp.float32)

    def three(part):
        return (
            dot(hi_ref[part], high[...]) + dot(hi_ref[part], low[...]) + dot(lo_ref[part], high[...])
        )

    width = o_ref.shape[3]
    by_real, by_imag = three(0), three(1)
    real = by_real[:, :width] - by_imag[:, width:]
    imag = by_real[:, width:] + by_imag[:, :width]
    for n in range(o_ref.shape[0]):
        o_ref[n, 0] = real[n * piece : (n + 1) * piece]
        o_ref[n, 1] = imag[n * piece : (n + 1) * piece]


def product(hi, lo, fill, rights, specs, count, width):
    _, rows, total = hi.shape
    piece = rows // count
    tile = min(512, rows)
    spec = pl.BlockSpec((2, tile, total), lambda m: (0, m, 0))
    return pl.pallas_call(
        functools.partial(product_kernel, fill),
        grid=(rows // tile,),
        out_shape=jax.ShapeDtypeStruct((count, 2, piece, width), jnp.float32),
        in_specs=[spec, spec] + specs,
        out_specs=pl.BlockSpec((tile // piece, 2, piece, width), lambda m: (m, 0, 0, 0)),
        scratch_shapes=[
            pltpu.VMEM((total, 2 * width), jnp.bfloat16),
            pltpu.VMEM((total, 2 * width), jnp.bfloat16),
        ],
        compiler_params=pltpu.CompilerParams(vmem_limit_bytes=VMEM),
        cost_estimate=pl.CostEstimate(
            flops=24 * rows * total * width,
            bytes_accessed=8 * rows * total + 16 * total * width + 8 * rows * width,
            transcendentals=0,
        ),
    )(hi, lo, *rights)


def place_kernel(stride, start, x_ref, *refs):
    o_ref, sems = refs[-2:]
    count, _, _, width = x_ref.shape
    copies = [
        pltpu.make_async_copy(
            x_ref.at[c], o_ref.at[:, :, pl.ds(c * stride + start, width)], sems.at[c]
        )
        for c in range(count)
    ]
    for copy in copies:
        copy.start()
    for copy in copies:
        copy.wait()


def place(received, out, start, cols):
    count, _, rows, _ = received.shape
    operands = [received] if out is None else [received, out]
    return pl.pallas_call(
        functools.partial(place_kernel, cols, start),
        out_shape=jax.ShapeDtypeStruct((2, rows, count * cols), jnp.float32),
        in_specs=[pl.BlockSpec(memory_space=pl.ANY)] * len(operands),
        out_specs=pl.BlockSpec(memory_space=pl.ANY),
        scratch_shapes=[pltpu.SemaphoreType.DMA((count,))],
        input_output_aliases={} if out is None else {1: 0},
        compiler_params=pltpu.CompilerParams(vmem_limit_bytes=VMEM),
        cost_estimate=pl.CostEstimate(
            flops=0, bytes_accessed=8 * received.size, transcendentals=0
        ),
    )(*operands)


def chunks_of(cols):
    start = 0
    for eighths in EIGHTHS:
        yield start, eighths * cols // 8
        start += eighths * cols // 8


def after(x, *others):
    return lax.optimization_barrier((x,) + others)[0]


def line_body(left, right, prefix_owner, qubit_order):
    z = lax.axis_index("row")
    me = lax.axis_index("col")
    count = lax.axis_size("col")
    _, rows, depth = left.shape
    _, deep, cols = right.shape
    hot = qubit_one_hot(qubit_order)
    core = (me % 2).reshape(1)
    chip = me // 2
    upper = (z >= 2).astype(jnp.int32)
    inner = jnp.logical_or(z == 1, z == 2)
    planes = jnp.stack([z, z ^ 1, 3 - z, (3 - z) ^ 1]).astype(jnp.int32)
    labels = jnp.arange(4, dtype=jnp.int32)
    slots = jnp.sum((planes[None, :] == labels[:, None]).astype(jnp.int32) * labels[None, :], axis=1)
    shards = jnp.stack([z, z ^ 1, 2 - upper, 3 - 3 * upper])
    table = jnp.concatenate([inner.astype(jnp.int32).reshape(1), chip ^ shards]).astype(jnp.int32)

    def along(x, pairs):
        return lax.ppermute(x, "row", pairs)

    turned = jnp.transpose(left, (0, 2, 1))
    halved, from_inner, from_end, landed = None, [], [], None
    for half in range(2):
        short, columns = depth // 2, cols // 2
        near = right[:, :, half * columns : (half + 1) * columns]
        if landed is not None:
            turned = after(turned, landed)
            near = after(near, landed)
        piece = turned[:, half * short : (half + 1) * short]
        mine = lax.dynamic_index_in_dim(piece, upper, 0, keepdims=False)
        theirs = lax.dynamic_index_in_dim(piece, 1 - upper, 0, keepdims=False)
        sources = [
            mine,
            along(mine, [(0, 1), (3, 2)]),
            along(theirs, [(1, 2), (2, 1)]),
            along(theirs, [(0, 2), (3, 1)]),
        ]
        early = along(near, [(1, 0), (2, 3)])
        *sources, early = lax.optimization_barrier((*sources, early))
        from_inner.append(early)
        kept, *sent = exchange_prefixes(sources, prefix_owner, planes, slots)
        near = after(near, kept)
        got = [
            along(sent[0], [(1, 0), (2, 3)]),
            along(sent[1], [(1, 2), (2, 1)]),
            along(sent[2], [(1, 3), (2, 0)]),
        ]
        early = along(near, [(0, 1), (3, 2)])
        kept, early, *got = lax.optimization_barrier((kept, early, *got, halved))[:5]
        from_end.append(early)
        real = lax.select_n(z, got[0], kept, got[1], got[2])
        imag = lax.select_n(z, got[2], got[1], kept, got[0])
        landed = jnp.stack([real, imag])
        halved = gather_left(landed, halved, half, hot, core)
    hi, lo = halved

    chunks = list(chunks_of(cols))
    across, forwarded, before = [], [], landed
    for start, width in chunks:
        half, offset = divmod(start, cols // 2)
        pair = jnp.stack(
            [
                right[:, :, start : start + width],
                from_end[half][:, :, offset : offset + width],
            ]
        )
        before = along(after(pair, before), [(1, 2), (2, 1)])
        across.append(before)
        forwarded.append(along(before, [(1, 0), (2, 3)]))

    out = None
    for n, (start, width) in enumerate(chunks):
        half, offset = divmod(start, cols // 2)
        whole = pl.BlockSpec((2, 2, deep, width), lambda m: (0, 0, 0, 0))

        def columns_at(start):
            return pl.BlockSpec((2, deep, width), lambda m: (0, 0, start // width))

        tile = product(
            hi,
            lo,
            fill_shards,
            [
                after(table, across[n + 1]) if n + 1 < len(chunks) else table,
                right,
                from_inner[half],
                from_end[half],
                across[n],
                forwarded[n],
            ],
            [
                pl.BlockSpec(memory_space=pltpu.SMEM),
                columns_at(start),
                columns_at(offset),
                columns_at(offset),
                whole,
                whole,
            ],
            count,
            width,
        )
        received = lax.all_to_all(tile, "col", split_axis=0, concat_axis=0, tiled=True)
        out = place(received, out, start, cols)
    return out


def any_body(left, right, prefix_owner, qubit_order):
    row_count = lax.axis_size("row")
    col_count = lax.axis_size("col")
    _, rows, depth = left.shape
    _, deep, cols = right.shape
    width = cols // 4
    inverse = owner_inverse(prefix_owner)
    hot = qubit_one_hot(qubit_order)

    turned = jnp.transpose(left, (0, 2, 1)).reshape(row_count, 2 * depth // row_count, rows)
    spread = lax.all_to_all(turned, "row", split_axis=0, concat_axis=0, tiled=True)
    ordered = order_prefixes(spread, inverse)
    landed = lax.all_to_all(ordered, "row", split_axis=0, concat_axis=0, tiled=True)
    gathered = lax.all_gather(landed.reshape(2, depth, rows), "col", axis=0)
    hi, lo = prepare_left(gathered, hot)

    out = None
    for start in range(0, cols, width):
        piece = right[:, :, start : start + width]
        whole = lax.all_gather(piece, "row", axis=0)
        spec = pl.BlockSpec((row_count, 2, deep, width), lambda m: (0, 0, 0, 0))
        tile = product(hi, lo, fill_whole, [whole], [spec], col_count, width)
        received = lax.all_to_all(tile, "col", split_axis=0, concat_axis=0, tiled=True)
        out = place(received, out, start, cols)
    return out


def solution(mesh):
    in_specs = (P(None, "row", "col"), P(None, "row", "col"), P(), P())
    out_specs = P(None, ("row", "col"), None)
    line = mesh.shape["row"] == 4 and mesh.shape["col"] == 8
    body = line_body if line else any_body
    return jax.shard_map(body, mesh=mesh, in_specs=in_specs, out_specs=out_specs, check_vma=False)
```

```python
import functools
import math

import jax
import jax.numpy as jnp
from jax import lax
from jax.experimental import pallas as pl
from jax.experimental.pallas import tpu as pltpu
from jax.sharding import PartitionSpec as P

LOW_BITS = 7
SPAN = 2**LOW_BITS
PREFIXES = 64
EIGHTHS = (2, 2, 2, 1, 1)
MIB = 2**20
VMEM = 58 * MIB


def owner_inverse(prefix_owner):
    labels = jnp.arange(PREFIXES, dtype=jnp.int32)
    match = (prefix_owner[None, :] == labels[:, None]).astype(jnp.int32)
    return jnp.sum(match * labels[None, :], axis=1)


def qubit_one_hot(qubit_order):
    offset = jnp.arange(SPAN, dtype=jnp.int32)
    bits = jnp.bitwise_and(jnp.right_shift(offset[:, None], qubit_order[None, :]), 1)
    powers = jnp.left_shift(jnp.ones((LOW_BITS,), jnp.int32), jnp.arange(LOW_BITS, dtype=jnp.int32))
    inner = jnp.sum(bits * powers[None, :], axis=1)
    return (inner[:, None] == offset[None, :]).astype(jnp.bfloat16)


def prefix_kernel(inverse_ref, x_ref, o_ref):
    per = x_ref.shape[2] // SPAN

    def move(o, _):
        p = inverse_ref[o]
        to = pl.multiple_of(lax.rem(o, per) * SPAN, SPAN)
        at = pl.multiple_of(lax.rem(p, per) * SPAN, SPAN)
        o_ref[o // per, :, pl.ds(to, SPAN)] = x_ref[p // per, :, pl.ds(at, SPAN)]
        return 0

    lax.fori_loop(0, PREFIXES, move, 0)


def order_prefixes(x, inverse):
    return pl.pallas_call(
        prefix_kernel,
        out_shape=jax.ShapeDtypeStruct(x.shape, x.dtype),
        in_specs=[
            pl.BlockSpec(memory_space=pltpu.SMEM),
            pl.BlockSpec(memory_space=pltpu.VMEM),
        ],
        out_specs=pl.BlockSpec(memory_space=pltpu.VMEM),
        compiler_params=pltpu.CompilerParams(vmem_limit_bytes=VMEM),
        cost_estimate=pl.CostEstimate(flops=0, bytes_accessed=8 * x.size, transcendentals=0),
    )(inverse, x)


def halves(x):
    hi = x.astype(jnp.bfloat16)
    return hi, (x - hi.astype(jnp.float32)).astype(jnp.bfloat16)


def left_kernel(hot_ref, x_ref, hi_ref, lo_ref):
    slices, _, depth, _ = x_ref.shape
    turn = functools.partial(
        lax.dot_general,
        dimension_numbers=(((1,), (1,)), ((), ())),
        preferred_element_type=jnp.float32,
    )
    for part in range(2):
        hi, lo = halves(x_ref[:, part].reshape(slices * depth, SPAN))
        hi_ref[part] = turn(hot_ref[...], hi).astype(jnp.bfloat16)
        lo_ref[part] = turn(hot_ref[...], lo).astype(jnp.bfloat16)


def prepare_left(gathered, hot):
    count, _, depth, rows = gathered.shape
    slices = 128 // math.gcd(depth, 128)
    half = jax.ShapeDtypeStruct((2, rows, count * depth), jnp.bfloat16)
    out_spec = pl.BlockSpec((2, SPAN, slices * depth), lambda j, c: (0, j, c))
    return pl.pallas_call(
        left_kernel,
        grid=(rows // SPAN, count // slices),
        out_shape=(half, half),
        in_specs=[
            pl.BlockSpec((SPAN, SPAN), lambda j, c: (0, 0)),
            pl.BlockSpec((slices, 2, depth, SPAN), lambda j, c: (c, 0, 0, j)),
        ],
        out_specs=(out_spec, out_spec),
        compiler_params=pltpu.CompilerParams(vmem_limit_bytes=VMEM),
        cost_estimate=pl.CostEstimate(
            flops=4 * gathered.size * SPAN, bytes_accessed=8 * gathered.size, transcendentals=0
        ),
    )(hot, gathered)


def exchange_kernel(owner_ref, planes_ref, slots_ref, *refs):
    sources, targets, held = refs[:4], refs[4:8], refs[8]
    per = sources[0].shape[1] // SPAN
    for s in range(4):
        for i in range(per):
            o = owner_ref[planes_ref[s] * per + i]
            to = pl.multiple_of(lax.rem(o, per) * SPAN, SPAN)
            held[slots_ref[o // per], :, pl.ds(to, SPAN)] = sources[s][:, i * SPAN : (i + 1) * SPAN]
    for s in range(4):
        targets[s][...] = held[s]


def exchange_prefixes(sources, prefix_owner, planes, slots):
    x = sources[0]
    vmem = pl.BlockSpec(memory_space=pltpu.VMEM)
    smem = pl.BlockSpec(memory_space=pltpu.SMEM)
    return pl.pallas_call(
        exchange_kernel,
        out_shape=[jax.ShapeDtypeStruct(x.shape, x.dtype)] * 4,
        in_specs=[smem] * 3 + [vmem] * 4,
        out_specs=[vmem] * 4,
        scratch_shapes=[pltpu.VMEM((4,) + x.shape, x.dtype)],
        compiler_params=pltpu.CompilerParams(vmem_limit_bytes=VMEM),
        cost_estimate=pl.CostEstimate(flops=0, bytes_accessed=32 * x.size, transcendentals=0),
    )(prefix_owner, planes, slots, *sources)


def slots_kernel(counts, core_ref, hot_ref, *refs):
    hi_ref, lo_ref = refs[-2:]
    even = core_ref[0] == 0
    for part in range(2):
        pieces = []
        at = 0
        for count in counts:
            if count == 1:
                mine, mate = refs[at][part], refs[at + 1][part]
            else:
                mine, mate = refs[at + part][...], refs[at + 2 + part][...]
            at += 2 * count
            pieces += [jnp.where(even, mine, mate), jnp.where(even, mate, mine)]
        hi, lo = halves(jnp.concatenate(pieces, axis=0))
        for n in range(hi.shape[1] // SPAN):
            span = slice(n * SPAN, (n + 1) * SPAN)
            for half, ref in ((hi, hi_ref), (lo, lo_ref)):
                ref[part, span] = lax.dot_general(
                    hot_ref[...],
                    half[:, span],
                    (((1,), (1,)), ((), ())),
                    preferred_element_type=jnp.float32,
                ).astype(jnp.bfloat16)


def prepare_slots(halved, block, blocks, hot, core, slots):
    counts, pieces = [], []
    for mine, mate in slots:
        counts.append(len(mine))
        pieces += list(mine) + list(mate)
    rows = pieces[0].shape[-1]
    wide = 2 * SPAN
    group = sum(2 * mine[0].shape[-2] for mine, _ in slots)
    half = jax.ShapeDtypeStruct((2, rows, blocks * group), jnp.bfloat16)
    in_specs = [pl.BlockSpec(memory_space=pltpu.SMEM), pl.BlockSpec((SPAN, SPAN), lambda j: (0, 0))]
    for x in pieces:
        if x.ndim == 3:
            in_specs.append(pl.BlockSpec(x.shape[:2] + (wide,), lambda j: (0, 0, j)))
        else:
            in_specs.append(pl.BlockSpec((x.shape[0], wide), lambda j: (0, j)))
    operands = [core, hot] + pieces
    aliases = {}
    if halved is not None:
        aliases = {len(operands): 0, len(operands) + 1: 1}
        in_specs += [pl.BlockSpec(memory_space=pl.ANY)] * 2
        operands += list(halved)
    out_spec = pl.BlockSpec((2, wide, group), lambda j: (0, j, block))
    return pl.pallas_call(
        functools.partial(slots_kernel, counts),
        grid=(rows // wide,),
        out_shape=(half, half),
        in_specs=in_specs,
        out_specs=(out_spec, out_spec),
        input_output_aliases=aliases,
        compiler_params=pltpu.CompilerParams(vmem_limit_bytes=VMEM),
        cost_estimate=pl.CostEstimate(flops=0, bytes_accessed=rows, transcendentals=0),
    )(*operands)


def swap(x, distance):
    count = lax.axis_size("col")
    return lax.ppermute(x, "col", [(i, i ^ distance) for i in range(count)])


def gather_left(held, halved, half, hot, core):
    own, along_x, along_y = held
    mate = swap(own, 1)
    mate_x = swap(along_x, 1)
    mate_y = swap(along_y, 1)
    corner = [along_x[0], along_y[1]]
    if half == 0:
        corner = lax.optimization_barrier((*corner, mate, mate_x, mate_y))[:2]
    corner = [swap(corner[0], 4), swap(corner[1], 2)]
    halved = prepare_slots(
        halved, 2 * half, 4, hot, core, [([own], [mate]), ([along_x], [mate_x])]
    )
    return halved, (along_y, mate_y, corner)


def gather_rest(rest, halved, half, hot, core):
    along_y, mate_y, corner = rest
    *corner, _ = lax.optimization_barrier((*corner, halved))
    mate_corner = [swap(x, 1) for x in corner]
    return prepare_slots(
        halved, 2 * half + 1, 4, hot, core, [([along_y], [mate_y]), (corner, mate_corner)]
    )


def put(high, low, part, at, x):
    width = x.shape[1]
    to = slice(part * width, (part + 1) * width)
    high[at, to], low[at, to] = halves(x)


def fill_whole(right_ref, high, low):
    shards, _, depth, _ = right_ref.shape
    for shard in range(shards):
        at = pl.ds(shard * depth, depth)
        for part in range(2):
            put(high, low, part, at, right_ref[shard, part])


def fill_shards(slot_ref, own_ref, near_ref, across, forwarded, high, low):
    depth = own_ref.shape[1]
    short = depth // 4

    def fill(slot, source):
        for part in range(2):
            for core in range(2):
                for half in range(2):
                    at = pl.multiple_of((half * 4 + slot) * 2 * short + core * short, 32)
                    k = core * 2 * short + half * short
                    put(high, low, part, pl.ds(at, short), source(part)[k : k + short])

    fill(slot_ref[1], lambda part: own_ref[part])
    fill(slot_ref[2], lambda part: near_ref[part])

    @pl.when(slot_ref[0] == 1)
    def _():
        for n in range(2):
            fill(slot_ref[3 + n], lambda part, n=n: across[n, part])

    @pl.when(slot_ref[0] == 0)
    def _():
        for n in range(2):
            fill(slot_ref[3 + n], lambda part, n=n: forwarded[n, part])


def product_kernel(fill, hi_ref, lo_ref, *refs):
    right_refs = refs[:-3]
    o_ref, high, low = refs[-3:]
    piece = o_ref.shape[2]

    @pl.when(pl.program_id(0) == 0)
    def _():
        fill(*right_refs, high, low)

    dot = functools.partial(jnp.dot, preferred_element_type=jnp.float32)

    def three(part):
        return (
            dot(hi_ref[part], high[...]) + dot(hi_ref[part], low[...]) + dot(lo_ref[part], high[...])
        )

    width = o_ref.shape[3]
    by_real, by_imag = three(0), three(1)
    real = by_real[:, :width] - by_imag[:, width:]
    imag = by_real[:, width:] + by_imag[:, :width]
    for n in range(o_ref.shape[0]):
        o_ref[n, 0] = real[n * piece : (n + 1) * piece]
        o_ref[n, 1] = imag[n * piece : (n + 1) * piece]


def product(hi, lo, fill, rights, specs, count, width):
    _, rows, total = hi.shape
    piece = rows // count
    tile = min(512, rows)
    spec = pl.BlockSpec((2, tile, total), lambda m: (0, m, 0))
    return pl.pallas_call(
        functools.partial(product_kernel, fill),
        grid=(rows // tile,),
        out_shape=jax.ShapeDtypeStruct((count, 2, piece, width), jnp.float32),
        in_specs=[spec, spec] + specs,
        out_specs=pl.BlockSpec((tile // piece, 2, piece, width), lambda m: (m, 0, 0, 0)),
        scratch_shapes=[
            pltpu.VMEM((total, 2 * width), jnp.bfloat16),
            pltpu.VMEM((total, 2 * width), jnp.bfloat16),
        ],
        compiler_params=pltpu.CompilerParams(vmem_limit_bytes=VMEM),
        cost_estimate=pl.CostEstimate(
            flops=24 * rows * total * width,
            bytes_accessed=8 * rows * total + 16 * total * width + 8 * rows * width,
            transcendentals=0,
        ),
    )(hi, lo, *rights)


def place_kernel(*refs):
    refs[-1][...] = refs[0][0]


def place(received, out, start, cols):
    count, _, rows, width = received.shape
    in_specs = [pl.BlockSpec((1, 2, rows, width), lambda c: (c, 0, 0, 0))]
    operands = [received]
    if out is not None:
        in_specs.append(pl.BlockSpec(memory_space=pl.ANY))
        operands.append(out)
    return pl.pallas_call(
        place_kernel,
        grid=(count,),
        out_shape=jax.ShapeDtypeStruct((2, rows, count * cols), jnp.float32),
        in_specs=in_specs,
        out_specs=pl.BlockSpec((2, rows, width), lambda c: (0, 0, (c * cols + start) // width)),
        input_output_aliases={} if out is None else {1: 0},
        compiler_params=pltpu.CompilerParams(vmem_limit_bytes=VMEM),
        cost_estimate=pl.CostEstimate(
            flops=0, bytes_accessed=8 * received.size, transcendentals=0
        ),
    )(*operands)


def chunks_of(cols):
    start = 0
    for eighths in EIGHTHS:
        yield start, eighths * cols // 8
        start += eighths * cols // 8


def after(x, *others):
    return lax.optimization_barrier((x,) + others)[0]


def line_body(left, right, prefix_owner, qubit_order):
    z = lax.axis_index("row")
    me = lax.axis_index("col")
    count = lax.axis_size("col")
    _, rows, depth = left.shape
    _, deep, cols = right.shape
    hot = qubit_one_hot(qubit_order)
    core = (me % 2).reshape(1)
    chip = me // 2
    upper = (z >= 2).astype(jnp.int32)
    inner = jnp.logical_or(z == 1, z == 2)
    planes = jnp.stack([z, z ^ 1, 3 - z, (3 - z) ^ 1]).astype(jnp.int32)
    labels = jnp.arange(4, dtype=jnp.int32)
    slots = jnp.sum((planes[None, :] == labels[:, None]).astype(jnp.int32) * labels[None, :], axis=1)
    shards = jnp.stack([z, z ^ 1, 2 - upper, 3 - 3 * upper])
    table = jnp.concatenate([inner.astype(jnp.int32).reshape(1), chip ^ shards]).astype(jnp.int32)

    def along(x, pairs):
        return lax.ppermute(x, "row", pairs)

    def along_line(pieces, pairs):
        return [along(*x) for x in zip(lax.optimization_barrier(pieces), pairs)]

    def segment(x, i):
        rows_of = x[:, i * deep // 4 : (i + 1) * deep // 4]
        return jnp.concatenate([rows_of[0], rows_of[1]], axis=1)

    to_neighbour = [(0, 1), (3, 2), (1, 0), (2, 3)]
    over_middle = [(1, 2), (2, 1)]
    turned = jnp.transpose(left, (0, 2, 1))
    shards_of, halved, near, landed, held = right, None, [], None, None
    for half in range(2):
        short = depth // 2
        if landed is not None:
            turned, shards_of, _ = lax.optimization_barrier((turned, right, landed))
        piece = turned[:, half * short : (half + 1) * short]
        mine = lax.dynamic_index_in_dim(piece, upper, 0, keepdims=False)
        theirs = lax.dynamic_index_in_dim(piece, 1 - upper, 0, keepdims=False)
        parts = [segment(shards_of, 2 * half), segment(shards_of, 2 * half + 1)]
        first = along_line(
            (jnp.where(inner, parts[0], mine), theirs, jnp.where(inner, parts[1], theirs)),
            (to_neighbour, over_middle, [(0, 2), (3, 1), (1, 0), (2, 3)]),
        )
        if held is not None:
            held = lax.optimization_barrier((*held, *first))[:3]
            halved, rest = gather_left(held, halved, half - 1, hot, core)
        kept, *sent = exchange_prefixes([mine] + first, prefix_owner, planes, slots)
        second = along_line(
            (jnp.where(inner, sent[0], parts[0]), sent[1], jnp.where(inner, sent[2], parts[1])),
            (to_neighbour, over_middle, [(1, 3), (2, 0), (0, 1), (3, 2)]),
        )
        if halved is not None:
            second, (halved, rest) = lax.optimization_barrier((second, (halved, rest)))
            halved = gather_rest(rest, halved, half - 1, hot, core)
        near += [jnp.where(inner, second[i], first[i]) for i in (0, 2)]
        real = lax.select_n(z, second[0], kept, second[1], second[2])
        imag = lax.select_n(z, second[2], second[1], kept, second[0])
        landed = jnp.stack([real, imag])
        held = (landed, swap(landed, 2), swap(landed, 4))
    held, halved = lax.optimization_barrier((held, halved))
    halved, rest = gather_left(held, halved, 1, hot, core)
    halved = gather_rest(rest, halved, 1, hot, core)
    near = jnp.stack(
        [jnp.concatenate([x[:, part * cols : (part + 1) * cols] for x in near]) for part in range(2)]
    )
    hi, lo = halved

    chunks = list(chunks_of(cols))
    across, forwarded = [], []
    for n, (start, width) in enumerate(chunks):
        pair = jnp.stack([x[:, :, start : start + width] for x in (right, near)])
        before = across[-1:] + forwarded[-2:-1] if n else [landed]
        across.append(along(after(pair, *before), over_middle))
        forwarded.append(along(across[-1], [(1, 0), (2, 3)]))

    out = None
    for n, (start, width) in enumerate(chunks):
        whole = pl.BlockSpec((2, 2, deep, width), lambda m: (0, 0, 0, 0))

        def columns_at(start):
            return pl.BlockSpec((2, deep, width), lambda m: (0, 0, start // width))

        tile = product(
            hi,
            lo,
            fill_shards,
            [
                after(table, across[n + 1]) if n + 1 < len(chunks) else table,
                right,
                near,
                across[n],
                forwarded[n],
            ],
            [
                pl.BlockSpec(memory_space=pltpu.SMEM),
                columns_at(start),
                columns_at(start),
                whole,
                whole,
            ],
            count,
            width,
        )
        received = lax.all_to_all(tile, "col", split_axis=0, concat_axis=0, tiled=True)
        out = place(received, out, start, cols)
    return out


def any_body(left, right, prefix_owner, qubit_order):
    row_count = lax.axis_size("row")
    col_count = lax.axis_size("col")
    _, rows, depth = left.shape
    _, deep, cols = right.shape
    width = cols // 4
    inverse = owner_inverse(prefix_owner)
    hot = qubit_one_hot(qubit_order)

    turned = jnp.transpose(left, (0, 2, 1)).reshape(row_count, 2 * depth // row_count, rows)
    spread = lax.all_to_all(turned, "row", split_axis=0, concat_axis=0, tiled=True)
    ordered = order_prefixes(spread, inverse)
    landed = lax.all_to_all(ordered, "row", split_axis=0, concat_axis=0, tiled=True)
    gathered = lax.all_gather(landed.reshape(2, depth, rows), "col", axis=0)
    hi, lo = prepare_left(gathered, hot)

    out = None
    for start in range(0, cols, width):
        piece = right[:, :, start : start + width]
        whole = lax.all_gather(piece, "row", axis=0)
        spec = pl.BlockSpec((row_count, 2, deep, width), lambda m: (0, 0, 0, 0))
        tile = product(hi, lo, fill_whole, [whole], [spec], col_count, width)
        received = lax.all_to_all(tile, "col", split_axis=0, concat_axis=0, tiled=True)
        out = place(received, out, start, cols)
    return out


def solution(mesh):
    in_specs = (P(None, "row", "col"), P(None, "row", "col"), P(), P())
    out_specs = P(None, ("row", "col"), None)
    line = mesh.shape["row"] == 4 and mesh.shape["col"] == 8
    body = line_body if line else any_body
    return jax.shard_map(body, mesh=mesh, in_specs=in_specs, out_specs=out_specs, check_vma=False)
```

```python
import functools
import math

import jax
import jax.numpy as jnp
from jax import lax
from jax.experimental import pallas as pl
from jax.experimental.pallas import tpu as pltpu
from jax.sharding import PartitionSpec as P

LOW_BITS = 7
SPAN = 2**LOW_BITS
PREFIXES = 64
EIGHTHS = (2, 2, 1, 1, 1, 1)
MIB = 2**20
VMEM = 58 * MIB


def owner_inverse(prefix_owner):
    labels = jnp.arange(PREFIXES, dtype=jnp.int32)
    match = (prefix_owner[None, :] == labels[:, None]).astype(jnp.int32)
    return jnp.sum(match * labels[None, :], axis=1)


def qubit_one_hot(qubit_order):
    offset = jnp.arange(SPAN, dtype=jnp.int32)
    bits = jnp.bitwise_and(jnp.right_shift(offset[:, None], qubit_order[None, :]), 1)
    powers = jnp.left_shift(jnp.ones((LOW_BITS,), jnp.int32), jnp.arange(LOW_BITS, dtype=jnp.int32))
    inner = jnp.sum(bits * powers[None, :], axis=1)
    return (inner[:, None] == offset[None, :]).astype(jnp.bfloat16)


def prefix_kernel(inverse_ref, x_ref, o_ref):
    per = x_ref.shape[2] // SPAN

    def move(o, _):
        p = inverse_ref[o]
        to = pl.multiple_of(lax.rem(o, per) * SPAN, SPAN)
        at = pl.multiple_of(lax.rem(p, per) * SPAN, SPAN)
        o_ref[o // per, :, pl.ds(to, SPAN)] = x_ref[p // per, :, pl.ds(at, SPAN)]
        return 0

    lax.fori_loop(0, PREFIXES, move, 0)


def order_prefixes(x, inverse):
    return pl.pallas_call(
        prefix_kernel,
        out_shape=jax.ShapeDtypeStruct(x.shape, x.dtype),
        in_specs=[
            pl.BlockSpec(memory_space=pltpu.SMEM),
            pl.BlockSpec(memory_space=pltpu.VMEM),
        ],
        out_specs=pl.BlockSpec(memory_space=pltpu.VMEM),
        compiler_params=pltpu.CompilerParams(vmem_limit_bytes=VMEM),
        cost_estimate=pl.CostEstimate(flops=0, bytes_accessed=8 * x.size, transcendentals=0),
    )(inverse, x)


def halves(x):
    hi = x.astype(jnp.bfloat16)
    return hi, (x - hi.astype(jnp.float32)).astype(jnp.bfloat16)


def left_kernel(hot_ref, x_ref, hi_ref, lo_ref):
    slices, _, depth, _ = x_ref.shape
    turn = functools.partial(
        lax.dot_general,
        dimension_numbers=(((1,), (1,)), ((), ())),
        preferred_element_type=jnp.float32,
    )
    for part in range(2):
        hi, lo = halves(x_ref[:, part].reshape(slices * depth, SPAN))
        hi_ref[part] = turn(hot_ref[...], hi).astype(jnp.bfloat16)
        lo_ref[part] = turn(hot_ref[...], lo).astype(jnp.bfloat16)


def prepare_left(gathered, hot):
    count, _, depth, rows = gathered.shape
    slices = 128 // math.gcd(depth, 128)
    half = jax.ShapeDtypeStruct((2, rows, count * depth), jnp.bfloat16)
    out_spec = pl.BlockSpec((2, SPAN, slices * depth), lambda j, c: (0, j, c))
    return pl.pallas_call(
        left_kernel,
        grid=(rows // SPAN, count // slices),
        out_shape=(half, half),
        in_specs=[
            pl.BlockSpec((SPAN, SPAN), lambda j, c: (0, 0)),
            pl.BlockSpec((slices, 2, depth, SPAN), lambda j, c: (c, 0, 0, j)),
        ],
        out_specs=(out_spec, out_spec),
        compiler_params=pltpu.CompilerParams(vmem_limit_bytes=VMEM),
        cost_estimate=pl.CostEstimate(
            flops=4 * gathered.size * SPAN, bytes_accessed=8 * gathered.size, transcendentals=0
        ),
    )(hot, gathered)


def exchange_kernel(owner_ref, planes_ref, slots_ref, *refs):
    sources, targets, held = refs[:4], refs[4:8], refs[8]
    per = sources[0].shape[1] // SPAN
    for s in range(4):
        for i in range(per):
            o = owner_ref[planes_ref[s] * per + i]
            to = pl.multiple_of(lax.rem(o, per) * SPAN, SPAN)
            held[slots_ref[o // per], :, pl.ds(to, SPAN)] = sources[s][:, i * SPAN : (i + 1) * SPAN]
    for s in range(4):
        targets[s][...] = held[s]


def exchange_prefixes(sources, prefix_owner, planes, slots):
    x = sources[0]
    vmem = pl.BlockSpec(memory_space=pltpu.VMEM)
    smem = pl.BlockSpec(memory_space=pltpu.SMEM)
    return pl.pallas_call(
        exchange_kernel,
        out_shape=[jax.ShapeDtypeStruct(x.shape, x.dtype)] * 4,
        in_specs=[smem] * 3 + [vmem] * 4,
        out_specs=[vmem] * 4,
        scratch_shapes=[pltpu.VMEM((4,) + x.shape, x.dtype)],
        compiler_params=pltpu.CompilerParams(vmem_limit_bytes=VMEM),
        cost_estimate=pl.CostEstimate(flops=0, bytes_accessed=32 * x.size, transcendentals=0),
    )(prefix_owner, planes, slots, *sources)


def slots_kernel(counts, core_ref, hot_ref, *refs):
    hi_ref, lo_ref = refs[-2:]
    even = core_ref[0] == 0
    for part in range(2):
        pieces = []
        at = 0
        for count in counts:
            if count == 1:
                mine, mate = refs[at][part], refs[at + 1][part]
            else:
                mine, mate = refs[at + part][...], refs[at + 2 + part][...]
            at += 2 * count
            pieces += [jnp.where(even, mine, mate), jnp.where(even, mate, mine)]
        hi, lo = halves(jnp.concatenate(pieces, axis=0))
        for n in range(hi.shape[1] // SPAN):
            span = slice(n * SPAN, (n + 1) * SPAN)
            for half, ref in ((hi, hi_ref), (lo, lo_ref)):
                ref[part, span] = lax.dot_general(
                    hot_ref[...],
                    half[:, span],
                    (((1,), (1,)), ((), ())),
                    preferred_element_type=jnp.float32,
                ).astype(jnp.bfloat16)


def prepare_slots(halved, block, blocks, hot, core, slots):
    counts, pieces = [], []
    for mine, mate in slots:
        counts.append(len(mine))
        pieces += list(mine) + list(mate)
    rows = pieces[0].shape[-1]
    wide = 2 * SPAN
    group = sum(2 * mine[0].shape[-2] for mine, _ in slots)
    half = jax.ShapeDtypeStruct((2, rows, blocks * group), jnp.bfloat16)
    in_specs = [pl.BlockSpec(memory_space=pltpu.SMEM), pl.BlockSpec((SPAN, SPAN), lambda j: (0, 0))]
    for x in pieces:
        if x.ndim == 3:
            in_specs.append(pl.BlockSpec(x.shape[:2] + (wide,), lambda j: (0, 0, j)))
        else:
            in_specs.append(pl.BlockSpec((x.shape[0], wide), lambda j: (0, j)))
    operands = [core, hot] + pieces
    aliases = {}
    if halved is not None:
        aliases = {len(operands): 0, len(operands) + 1: 1}
        in_specs += [pl.BlockSpec(memory_space=pl.ANY)] * 2
        operands += list(halved)
    out_spec = pl.BlockSpec((2, wide, group), lambda j: (0, j, block))
    return pl.pallas_call(
        functools.partial(slots_kernel, counts),
        grid=(rows // wide,),
        out_shape=(half, half),
        in_specs=in_specs,
        out_specs=(out_spec, out_spec),
        input_output_aliases=aliases,
        compiler_params=pltpu.CompilerParams(vmem_limit_bytes=VMEM),
        cost_estimate=pl.CostEstimate(flops=0, bytes_accessed=rows * (16 * group if block == blocks - 1 else 1), transcendentals=0),
    )(*operands)


def swap(x, distance):
    count = lax.axis_size("col")
    return lax.ppermute(x, "col", [(i, i ^ distance) for i in range(count)])


def gather_left(held, halved, half, hot, core):
    own, along_x, along_y = held
    mate = swap(own, 1)
    mate_x = swap(along_x, 1)
    mate_y = swap(along_y, 1)
    corner = [along_x[0], along_y[1]]
    if half == 0:
        corner = lax.optimization_barrier((*corner, mate, mate_x, mate_y))[:2]
    corner = [swap(corner[0], 4), swap(corner[1], 2)]
    halved = prepare_slots(
        halved, 2 * half, 4, hot, core, [([own], [mate]), ([along_x], [mate_x])]
    )
    return halved, (along_y, mate_y, corner)


def gather_rest(rest, halved, half, hot, core):
    along_y, mate_y, corner = rest
    *corner, _ = lax.optimization_barrier((*corner, halved))
    mate_corner = [swap(x, 1) for x in corner]
    return prepare_slots(
        halved, 2 * half + 1, 4, hot, core, [([along_y], [mate_y]), (corner, mate_corner)]
    )


def put(high, low, part, at, x):
    width = x.shape[1]
    to = slice(part * width, (part + 1) * width)
    high[at, to], low[at, to] = halves(x)


def fill_whole(right_ref, high, low):
    shards, _, depth, _ = right_ref.shape
    for shard in range(shards):
        at = pl.ds(shard * depth, depth)
        for part in range(2):
            put(high, low, part, at, right_ref[shard, part])


def fill_shards(slot_ref, own_ref, near_ref, across, forwarded, high, low):
    depth = own_ref.shape[1]
    short = depth // 4

    def fill(slot, source):
        for part in range(2):
            for core in range(2):
                for half in range(2):
                    at = pl.multiple_of((half * 4 + slot) * 2 * short + core * short, 32)
                    k = core * 2 * short + half * short
                    put(high, low, part, pl.ds(at, short), source(part)[k : k + short])

    fill(slot_ref[1], lambda part: own_ref[part])
    fill(slot_ref[2], lambda part: near_ref[part])

    @pl.when(slot_ref[0] == 1)
    def _():
        for n in range(2):
            fill(slot_ref[3 + n], lambda part, n=n: across[n, part])

    @pl.when(slot_ref[0] == 0)
    def _():
        for n in range(2):
            fill(slot_ref[3 + n], lambda part, n=n: forwarded[n, part])


def product_kernel(fill, hi_ref, lo_ref, *refs):
    right_refs = refs[:-3]
    o_ref, high, low = refs[-3:]
    piece = o_ref.shape[2]

    @pl.when(pl.program_id(0) == 0)
    def _():
        fill(*right_refs, high, low)

    dot = functools.partial(jnp.dot, preferred_element_type=jnp.float32)

    def three(part):
        return (
            dot(hi_ref[part], high[...]) + dot(hi_ref[part], low[...]) + dot(lo_ref[part], high[...])
        )

    width = o_ref.shape[3]
    by_real, by_imag = three(0), three(1)
    real = by_real[:, :width] - by_imag[:, width:]
    imag = by_real[:, width:] + by_imag[:, :width]
    for n in range(o_ref.shape[0]):
        o_ref[n, 0] = real[n * piece : (n + 1) * piece]
        o_ref[n, 1] = imag[n * piece : (n + 1) * piece]


def product(hi, lo, fill, rights, specs, count, width):
    _, rows, total = hi.shape
    piece = rows // count
    tile = min(512, rows)
    spec = pl.BlockSpec((2, tile, total), lambda m: (0, m, 0))
    return pl.pallas_call(
        functools.partial(product_kernel, fill),
        grid=(rows // tile,),
        out_shape=jax.ShapeDtypeStruct((count, 2, piece, width), jnp.float32),
        in_specs=[spec, spec] + specs,
        out_specs=pl.BlockSpec((tile // piece, 2, piece, width), lambda m: (m, 0, 0, 0)),
        scratch_shapes=[
            pltpu.VMEM((total, 2 * width), jnp.bfloat16),
            pltpu.VMEM((total, 2 * width), jnp.bfloat16),
        ],
        compiler_params=pltpu.CompilerParams(vmem_limit_bytes=VMEM),
        cost_estimate=pl.CostEstimate(flops=0, bytes_accessed=rows, transcendentals=0),
    )(hi, lo, *rights)


def place_kernel(count, *refs):
    start = 0
    for ref in refs[:count]:
        width = ref.shape[3]
        refs[-1][:, :, start : start + width] = ref[0]
        start += width


def place(received, out, start, cols):
    count, _, rows, _ = received[0].shape
    width = sum(x.shape[3] for x in received)
    in_specs = [pl.BlockSpec((1,) + x.shape[1:], lambda c: (c, 0, 0, 0)) for x in received]
    operands = list(received)
    if out is not None:
        in_specs.append(pl.BlockSpec(memory_space=pl.ANY))
        operands.append(out)
    return pl.pallas_call(
        functools.partial(place_kernel, len(received)),
        grid=(count,),
        out_shape=jax.ShapeDtypeStruct((2, rows, count * cols), jnp.float32),
        in_specs=in_specs,
        out_specs=pl.BlockSpec((2, rows, width), lambda c: (0, 0, (c * cols + start) // width)),
        input_output_aliases={} if out is None else {len(received): 0},
        compiler_params=pltpu.CompilerParams(vmem_limit_bytes=VMEM),
        cost_estimate=pl.CostEstimate(
            flops=0, bytes_accessed=8 * count * rows * 2 * width, transcendentals=0
        ),
    )(*operands)


def chunks_of(cols):
    start = 0
    for eighths in EIGHTHS:
        yield start, eighths * cols // 8
        start += eighths * cols // 8


def after(x, *others):
    return lax.optimization_barrier((x,) + others)[0]


def line_body(left, right, prefix_owner, qubit_order):
    z = lax.axis_index("row")
    me = lax.axis_index("col")
    count = lax.axis_size("col")
    _, rows, depth = left.shape
    _, deep, cols = right.shape
    hot = qubit_one_hot(qubit_order)
    core = (me % 2).reshape(1)
    chip = me // 2
    upper = (z >= 2).astype(jnp.int32)
    inner = jnp.logical_or(z == 1, z == 2)
    planes = jnp.stack([z, z ^ 1, 3 - z, (3 - z) ^ 1]).astype(jnp.int32)
    labels = jnp.arange(4, dtype=jnp.int32)
    slots = jnp.sum((planes[None, :] == labels[:, None]).astype(jnp.int32) * labels[None, :], axis=1)
    shards = jnp.stack([z, z ^ 1, 2 - upper, 3 - 3 * upper])
    table = jnp.concatenate([inner.astype(jnp.int32).reshape(1), chip ^ shards]).astype(jnp.int32)

    def along(x, pairs):
        return lax.ppermute(x, "row", pairs)

    def along_line(pieces, pairs):
        return [along(*x) for x in zip(lax.optimization_barrier(pieces), pairs)]

    def segment(x, i):
        rows_of = x[:, i * deep // 4 : (i + 1) * deep // 4]
        return jnp.concatenate([rows_of[0], rows_of[1]], axis=1)

    to_neighbour = [(0, 1), (3, 2), (1, 0), (2, 3)]
    over_middle = [(1, 2), (2, 1)]
    turned = jnp.transpose(left, (0, 2, 1))
    halved, near, held, second = None, [], None, None
    for half in range(2):
        short = depth // 2
        piece = turned[:, half * short : (half + 1) * short]
        mine = lax.dynamic_index_in_dim(piece, upper, 0, keepdims=False)
        theirs = lax.dynamic_index_in_dim(piece, 1 - upper, 0, keepdims=False)
        parts = [segment(right, 2 * half), segment(right, 2 * half + 1)]
        pieces = (jnp.where(inner, parts[0], mine), theirs, jnp.where(inner, parts[1], theirs))
        if half:
            pieces, second = lax.optimization_barrier((pieces, second))
        first = along_line(
            pieces,
            (to_neighbour, over_middle, [(0, 2), (3, 1), (1, 0), (2, 3)]),
        )
        if held is not None:
            held = lax.optimization_barrier((*held, *first))[:3]
            halved, rest = gather_left(held, halved, half - 1, hot, core)
        kept, *sent = exchange_prefixes([mine] + first, prefix_owner, planes, slots)
        second = along_line(
            (jnp.where(inner, sent[0], parts[0]), sent[1], jnp.where(inner, sent[2], parts[1])),
            (to_neighbour, over_middle, [(1, 3), (2, 0), (0, 1), (3, 2)]),
        )
        if halved is not None:
            second, (halved, rest) = lax.optimization_barrier((second, (halved, rest)))
            halved = gather_rest(rest, halved, half - 1, hot, core)
        near += [jnp.where(inner, second[i], first[i]) for i in (0, 2)]
        real = lax.select_n(z, second[0], kept, second[1], second[2])
        imag = lax.select_n(z, second[2], second[1], kept, second[0])
        landed = jnp.stack([real, imag])
        held = (landed, swap(landed, 2), swap(landed, 4))
    held, halved = lax.optimization_barrier((held, halved))
    halved, rest = gather_left(held, halved, 1, hot, core)
    halved = gather_rest(rest, halved, 1, hot, core)
    near = jnp.stack(
        [jnp.concatenate([x[:, part * cols : (part + 1) * cols] for x in near]) for part in range(2)]
    )
    hi, lo = halved

    chunks = list(chunks_of(cols))
    across, forwarded = [], []
    for n, (start, width) in enumerate(chunks):
        pair = jnp.stack([x[:, :, start : start + width] for x in (right, near)])
        before = across[-1:] + forwarded[-2:-1] if n else [landed]
        across.append(along(after(pair, *before), over_middle))
        forwarded.append(along(across[-1], [(1, 0), (2, 3)]))

    out, tile, waiting = None, None, []
    for n, (start, width) in enumerate(chunks):
        earlier = across[n + 1 : n + 2] + ([] if tile is None else [tile])
        whole = pl.BlockSpec((2, 2, deep, width), lambda m: (0, 0, 0, 0))

        def columns_at(start):
            return pl.BlockSpec((2, deep, width), lambda m: (0, 0, start // width))

        tile = product(
            hi,
            lo,
            fill_shards,
            [
                after(table, *earlier),
                right,
                near,
                across[n],
                forwarded[n],
            ],
            [
                pl.BlockSpec(memory_space=pltpu.SMEM),
                columns_at(start),
                columns_at(start),
                whole,
                whole,
            ],
            count,
            width,
        )
        received = lax.all_to_all(tile, "col", split_axis=0, concat_axis=0, tiled=True)
        waiting.append(received)
        if n % 2:
            out = place(waiting, out, start - waiting[0].shape[3], cols)
            waiting = []
    return out


def any_body(left, right, prefix_owner, qubit_order):
    row_count = lax.axis_size("row")
    col_count = lax.axis_size("col")
    _, rows, depth = left.shape
    _, deep, cols = right.shape
    width = cols // 4
    inverse = owner_inverse(prefix_owner)
    hot = qubit_one_hot(qubit_order)

    turned = jnp.transpose(left, (0, 2, 1)).reshape(row_count, 2 * depth // row_count, rows)
    spread = lax.all_to_all(turned, "row", split_axis=0, concat_axis=0, tiled=True)
    ordered = order_prefixes(spread, inverse)
    landed = lax.all_to_all(ordered, "row", split_axis=0, concat_axis=0, tiled=True)
    gathered = lax.all_gather(landed.reshape(2, depth, rows), "col", axis=0)
    hi, lo = prepare_left(gathered, hot)

    out = None
    for start in range(0, cols, width):
        piece = right[:, :, start : start + width]
        whole = lax.all_gather(piece, "row", axis=0)
        spec = pl.BlockSpec((row_count, 2, deep, width), lambda m: (0, 0, 0, 0))
        tile = product(hi, lo, fill_whole, [whole], [spec], col_count, width)
        received = lax.all_to_all(tile, "col", split_axis=0, concat_axis=0, tiled=True)
        out = place([received], out, start, cols)
    return out


def solution(mesh):
    in_specs = (P(None, "row", "col"), P(None, "row", "col"), P(), P())
    out_specs = P(None, ("row", "col"), None)
    line = mesh.shape["row"] == 4 and mesh.shape["col"] == 8
    body = line_body if line else any_body
    return jax.shard_map(body, mesh=mesh, in_specs=in_specs, out_specs=out_specs, check_vma=False)
```

```python
import functools
import math

import jax
import jax.numpy as jnp
from jax import lax
from jax.experimental import pallas as pl
from jax.experimental.pallas import tpu as pltpu
from jax.sharding import PartitionSpec as P

LOW_BITS = 7
SPAN = 2**LOW_BITS
PREFIXES = 64
EIGHTHS = (2, 2, 2, 2)
MIB = 2**20
VMEM = 58 * MIB


def owner_inverse(prefix_owner):
    labels = jnp.arange(PREFIXES, dtype=jnp.int32)
    match = (prefix_owner[None, :] == labels[:, None]).astype(jnp.int32)
    return jnp.sum(match * labels[None, :], axis=1)


def qubit_one_hot(qubit_order):
    offset = jnp.arange(SPAN, dtype=jnp.int32)
    bits = jnp.bitwise_and(jnp.right_shift(offset[:, None], qubit_order[None, :]), 1)
    powers = jnp.left_shift(jnp.ones((LOW_BITS,), jnp.int32), jnp.arange(LOW_BITS, dtype=jnp.int32))
    inner = jnp.sum(bits * powers[None, :], axis=1)
    return (inner[:, None] == offset[None, :]).astype(jnp.bfloat16)


def prefix_kernel(inverse_ref, x_ref, o_ref):
    per = x_ref.shape[2] // SPAN

    def move(o, _):
        p = inverse_ref[o]
        to = pl.multiple_of(lax.rem(o, per) * SPAN, SPAN)
        at = pl.multiple_of(lax.rem(p, per) * SPAN, SPAN)
        o_ref[o // per, :, pl.ds(to, SPAN)] = x_ref[p // per, :, pl.ds(at, SPAN)]
        return 0

    lax.fori_loop(0, PREFIXES, move, 0)


def order_prefixes(x, inverse):
    return pl.pallas_call(
        prefix_kernel,
        out_shape=jax.ShapeDtypeStruct(x.shape, x.dtype),
        in_specs=[
            pl.BlockSpec(memory_space=pltpu.SMEM),
            pl.BlockSpec(memory_space=pltpu.VMEM),
        ],
        out_specs=pl.BlockSpec(memory_space=pltpu.VMEM),
        compiler_params=pltpu.CompilerParams(vmem_limit_bytes=VMEM),
        cost_estimate=pl.CostEstimate(flops=0, bytes_accessed=8 * x.size, transcendentals=0),
    )(inverse, x)


def halves(x):
    hi = x.astype(jnp.bfloat16)
    return hi, (x - hi.astype(jnp.float32)).astype(jnp.bfloat16)


def left_kernel(hot_ref, x_ref, hi_ref, lo_ref):
    slices, _, depth, _ = x_ref.shape
    turn = functools.partial(
        lax.dot_general,
        dimension_numbers=(((1,), (1,)), ((), ())),
        preferred_element_type=jnp.float32,
    )
    for part in range(2):
        hi, lo = halves(x_ref[:, part].reshape(slices * depth, SPAN))
        hi_ref[part] = turn(hot_ref[...], hi).astype(jnp.bfloat16)
        lo_ref[part] = turn(hot_ref[...], lo).astype(jnp.bfloat16)


def prepare_left(gathered, hot):
    count, _, depth, rows = gathered.shape
    slices = 128 // math.gcd(depth, 128)
    half = jax.ShapeDtypeStruct((2, rows, count * depth), jnp.bfloat16)
    out_spec = pl.BlockSpec((2, SPAN, slices * depth), lambda j, c: (0, j, c))
    return pl.pallas_call(
        left_kernel,
        grid=(rows // SPAN, count // slices),
        out_shape=(half, half),
        in_specs=[
            pl.BlockSpec((SPAN, SPAN), lambda j, c: (0, 0)),
            pl.BlockSpec((slices, 2, depth, SPAN), lambda j, c: (c, 0, 0, j)),
        ],
        out_specs=(out_spec, out_spec),
        compiler_params=pltpu.CompilerParams(vmem_limit_bytes=VMEM),
        cost_estimate=pl.CostEstimate(
            flops=4 * gathered.size * SPAN, bytes_accessed=8 * gathered.size, transcendentals=0
        ),
    )(hot, gathered)


def exchange_kernel(owner_ref, planes_ref, slots_ref, *refs):
    sources, targets, held = refs[:4], refs[4:8], refs[8]
    per = sources[0].shape[1] // SPAN
    for s in range(4):
        for i in range(per):
            o = owner_ref[planes_ref[s] * per + i]
            to = pl.multiple_of(lax.rem(o, per) * SPAN, SPAN)
            held[slots_ref[o // per], :, pl.ds(to, SPAN)] = sources[s][:, i * SPAN : (i + 1) * SPAN]
    for s in range(4):
        targets[s][...] = held[s]


def exchange_prefixes(sources, prefix_owner, planes, slots):
    x = sources[0]
    vmem = pl.BlockSpec(memory_space=pltpu.VMEM)
    smem = pl.BlockSpec(memory_space=pltpu.SMEM)
    return pl.pallas_call(
        exchange_kernel,
        out_shape=[jax.ShapeDtypeStruct(x.shape, x.dtype)] * 4,
        in_specs=[smem] * 3 + [vmem] * 4,
        out_specs=[vmem] * 4,
        scratch_shapes=[pltpu.VMEM((4,) + x.shape, x.dtype)],
        compiler_params=pltpu.CompilerParams(vmem_limit_bytes=VMEM),
        cost_estimate=pl.CostEstimate(flops=0, bytes_accessed=32 * x.size, transcendentals=0),
    )(prefix_owner, planes, slots, *sources)


def slots_kernel(counts, core_ref, hot_ref, *refs):
    hi_ref, lo_ref = refs[-2:]
    even = core_ref[0] == 0
    for part in range(2):
        pieces = []
        at = 0
        for count in counts:
            if count == 1:
                mine, mate = refs[at][part], refs[at + 1][part]
            else:
                mine, mate = refs[at + part][...], refs[at + 2 + part][...]
            at += 2 * count
            pieces += [jnp.where(even, mine, mate), jnp.where(even, mate, mine)]
        hi, lo = halves(jnp.concatenate(pieces, axis=0))
        for n in range(hi.shape[1] // SPAN):
            span = slice(n * SPAN, (n + 1) * SPAN)
            for half, ref in ((hi, hi_ref), (lo, lo_ref)):
                ref[part, span] = lax.dot_general(
                    hot_ref[...],
                    half[:, span],
                    (((1,), (1,)), ((), ())),
                    preferred_element_type=jnp.float32,
                ).astype(jnp.bfloat16)


def prepare_slots(halved, block, blocks, hot, core, slots):
    counts, pieces = [], []
    for mine, mate in slots:
        counts.append(len(mine))
        pieces += list(mine) + list(mate)
    rows = pieces[0].shape[-1]
    wide = 2 * SPAN
    group = sum(2 * mine[0].shape[-2] for mine, _ in slots)
    half = jax.ShapeDtypeStruct((2, rows, blocks * group), jnp.bfloat16)
    in_specs = [pl.BlockSpec(memory_space=pltpu.SMEM), pl.BlockSpec((SPAN, SPAN), lambda j: (0, 0))]
    for x in pieces:
        if x.ndim == 3:
            in_specs.append(pl.BlockSpec(x.shape[:2] + (wide,), lambda j: (0, 0, j)))
        else:
            in_specs.append(pl.BlockSpec((x.shape[0], wide), lambda j: (0, j)))
    operands = [core, hot] + pieces
    aliases = {}
    if halved is not None:
        aliases = {len(operands): 0, len(operands) + 1: 1}
        in_specs += [pl.BlockSpec(memory_space=pl.ANY)] * 2
        operands += list(halved)
    out_spec = pl.BlockSpec((2, wide, group), lambda j: (0, j, block))
    return pl.pallas_call(
        functools.partial(slots_kernel, counts),
        grid=(rows // wide,),
        out_shape=(half, half),
        in_specs=in_specs,
        out_specs=(out_spec, out_spec),
        input_output_aliases=aliases,
        compiler_params=pltpu.CompilerParams(vmem_limit_bytes=VMEM),
        cost_estimate=pl.CostEstimate(flops=0, bytes_accessed=rows * (16 * group if block == blocks - 1 else 1), transcendentals=0),
    )(*operands)


def swap(x, distance):
    count = lax.axis_size("col")
    return lax.ppermute(x, "col", [(i, i ^ distance) for i in range(count)])


def gather_left(held, halved, half, hot, core):
    own, along_x, along_y = held
    mate = swap(own, 1)
    mate_x = swap(along_x, 1)
    mate_y = swap(along_y, 1)
    corner = [along_x[0], along_y[1]]
    if half == 0:
        corner = lax.optimization_barrier((*corner, mate, mate_x, mate_y))[:2]
    corner = [swap(corner[0], 4), swap(corner[1], 2)]
    halved = prepare_slots(
        halved, 2 * half, 4, hot, core, [([own], [mate]), ([along_x], [mate_x])]
    )
    return halved, (along_y, mate_y, corner)


def gather_rest(rest, halved, half, hot, core):
    along_y, mate_y, corner = rest
    *corner, _ = lax.optimization_barrier((*corner, halved))
    mate_corner = [swap(x, 1) for x in corner]
    return prepare_slots(
        halved, 2 * half + 1, 4, hot, core, [([along_y], [mate_y]), (corner, mate_corner)]
    )


def put(high, low, part, at, x):
    width = x.shape[1]
    to = slice(part * width, (part + 1) * width)
    high[at, to], low[at, to] = halves(x)


def fill_whole(right_ref, high, low):
    shards, _, depth, _ = right_ref.shape
    for shard in range(shards):
        at = pl.ds(shard * depth, depth)
        for part in range(2):
            put(high, low, part, at, right_ref[shard, part])


def fill_shards(slot_ref, own_ref, near_ref, across, forwarded, high, low):
    depth = own_ref.shape[1]
    short = depth // 4

    def fill(slot, source):
        for part in range(2):
            for core in range(2):
                for half in range(2):
                    at = pl.multiple_of((half * 4 + slot) * 2 * short + core * short, 32)
                    k = core * 2 * short + half * short
                    put(high, low, part, pl.ds(at, short), source(part)[k : k + short])

    fill(slot_ref[1], lambda part: own_ref[part])
    fill(slot_ref[2], lambda part: near_ref[part])

    @pl.when(slot_ref[0] == 1)
    def _():
        for n in range(2):
            fill(slot_ref[3 + n], lambda part, n=n: across[n, part])

    @pl.when(slot_ref[0] == 0)
    def _():
        for n in range(2):
            fill(slot_ref[3 + n], lambda part, n=n: forwarded[n, part])


def product_kernel(fill, hi_ref, lo_ref, *refs):
    right_refs = refs[:-3]
    o_ref, high, low = refs[-3:]
    piece = o_ref.shape[2]

    @pl.when(pl.program_id(0) == 0)
    def _():
        fill(*right_refs, high, low)

    dot = functools.partial(jnp.dot, preferred_element_type=jnp.float32)

    def three(part):
        return (
            dot(hi_ref[part], high[...]) + dot(hi_ref[part], low[...]) + dot(lo_ref[part], high[...])
        )

    width = o_ref.shape[3]
    by_real, by_imag = three(0), three(1)
    real = by_real[:, :width] - by_imag[:, width:]
    imag = by_real[:, width:] + by_imag[:, :width]
    for n in range(o_ref.shape[0]):
        o_ref[n, 0] = real[n * piece : (n + 1) * piece]
        o_ref[n, 1] = imag[n * piece : (n + 1) * piece]


def product(hi, lo, fill, rights, specs, count, width):
    _, rows, total = hi.shape
    piece = rows // count
    tile = min(512, rows)
    spec = pl.BlockSpec((2, tile, total), lambda m: (0, m, 0))
    return pl.pallas_call(
        functools.partial(product_kernel, fill),
        grid=(rows // tile,),
        out_shape=jax.ShapeDtypeStruct((count, 2, piece, width), jnp.float32),
        in_specs=[spec, spec] + specs,
        out_specs=pl.BlockSpec((tile // piece, 2, piece, width), lambda m: (m, 0, 0, 0)),
        scratch_shapes=[
            pltpu.VMEM((total, 2 * width), jnp.bfloat16),
            pltpu.VMEM((total, 2 * width), jnp.bfloat16),
        ],
        compiler_params=pltpu.CompilerParams(vmem_limit_bytes=VMEM),
        cost_estimate=pl.CostEstimate(
            flops=24 * rows * total * width,
            bytes_accessed=8 * rows * total + 16 * total * width + 8 * rows * width,
            transcendentals=0,
        ),
    )(hi, lo, *rights)


def place_kernel(count, *refs):
    start = 0
    for ref in refs[:count]:
        width = ref.shape[3]
        refs[-1][:, :, start : start + width] = ref[0]
        start += width


def place(received, out, start, cols):
    count, _, rows, _ = received[0].shape
    width = sum(x.shape[3] for x in received)
    in_specs = [pl.BlockSpec((1,) + x.shape[1:], lambda c: (c, 0, 0, 0)) for x in received]
    operands = list(received)
    if out is not None:
        in_specs.append(pl.BlockSpec(memory_space=pl.ANY))
        operands.append(out)
    return pl.pallas_call(
        functools.partial(place_kernel, len(received)),
        grid=(count,),
        out_shape=jax.ShapeDtypeStruct((2, rows, count * cols), jnp.float32),
        in_specs=in_specs,
        out_specs=pl.BlockSpec((2, rows, width), lambda c: (0, 0, (c * cols + start) // width)),
        input_output_aliases={} if out is None else {len(received): 0},
        compiler_params=pltpu.CompilerParams(vmem_limit_bytes=VMEM),
        cost_estimate=pl.CostEstimate(
            flops=0, bytes_accessed=8 * count * rows * 2 * width, transcendentals=0
        ),
    )(*operands)


def chunks_of(cols):
    start = 0
    for eighths in EIGHTHS:
        yield start, eighths * cols // 8
        start += eighths * cols // 8


def after(x, *others):
    return lax.optimization_barrier((x,) + others)[0]


def line_body(left, right, prefix_owner, qubit_order):
    z = lax.axis_index("row")
    me = lax.axis_index("col")
    count = lax.axis_size("col")
    _, rows, depth = left.shape
    _, deep, cols = right.shape
    hot = qubit_one_hot(qubit_order)
    core = (me % 2).reshape(1)
    chip = me // 2
    upper = (z >= 2).astype(jnp.int32)
    inner = jnp.logical_or(z == 1, z == 2)
    planes = jnp.stack([z, z ^ 1, 3 - z, (3 - z) ^ 1]).astype(jnp.int32)
    labels = jnp.arange(4, dtype=jnp.int32)
    slots = jnp.sum((planes[None, :] == labels[:, None]).astype(jnp.int32) * labels[None, :], axis=1)
    shards = jnp.stack([z, z ^ 1, 2 - upper, 3 - 3 * upper])
    table = jnp.concatenate([inner.astype(jnp.int32).reshape(1), chip ^ shards]).astype(jnp.int32)

    def along(x, pairs):
        return lax.ppermute(x, "row", pairs)

    def along_line(pieces, pairs):
        return [along(*x) for x in zip(lax.optimization_barrier(pieces), pairs)]

    def segment(x, i):
        rows_of = x[:, i * deep // 4 : (i + 1) * deep // 4]
        return jnp.concatenate([rows_of[0], rows_of[1]], axis=1)

    to_neighbour = [(0, 1), (3, 2), (1, 0), (2, 3)]
    over_middle = [(1, 2), (2, 1)]
    turned = jnp.transpose(left, (0, 2, 1))
    halved, near, held, second = None, [], None, None
    for half in range(2):
        short = depth // 2
        piece = turned[:, half * short : (half + 1) * short]
        mine = lax.dynamic_index_in_dim(piece, upper, 0, keepdims=False)
        theirs = lax.dynamic_index_in_dim(piece, 1 - upper, 0, keepdims=False)
        parts = [segment(right, 2 * half), segment(right, 2 * half + 1)]
        pieces = (jnp.where(inner, parts[0], mine), theirs, jnp.where(inner, parts[1], theirs))
        if half:
            pieces, second = lax.optimization_barrier((pieces, second))
        first = along_line(
            pieces,
            (to_neighbour, over_middle, [(0, 2), (3, 1), (1, 0), (2, 3)]),
        )
        if held is not None:
            held = lax.optimization_barrier((*held, *first))[:3]
            halved, rest = gather_left(held, halved, half - 1, hot, core)
        kept, *sent = exchange_prefixes([mine] + first, prefix_owner, planes, slots)
        second = along_line(
            (jnp.where(inner, sent[0], parts[0]), sent[1], jnp.where(inner, sent[2], parts[1])),
            (to_neighbour, over_middle, [(1, 3), (2, 0), (0, 1), (3, 2)]),
        )
        if halved is not None:
            second, (halved, rest) = lax.optimization_barrier((second, (halved, rest)))
            halved = gather_rest(rest, halved, half - 1, hot, core)
        near += [jnp.where(inner, second[i], first[i]) for i in (0, 2)]
        real = lax.select_n(z, second[0], kept, second[1], second[2])
        imag = lax.select_n(z, second[2], second[1], kept, second[0])
        landed = jnp.stack([real, imag])
        held = (landed, swap(landed, 2), swap(landed, 4))
    held, halved = lax.optimization_barrier((held, halved))
    halved, rest = gather_left(held, halved, 1, hot, core)
    halved = gather_rest(rest, halved, 1, hot, core)
    near = jnp.stack(
        [jnp.concatenate([x[:, part * cols : (part + 1) * cols] for x in near]) for part in range(2)]
    )
    hi, lo = halved

    chunks = list(chunks_of(cols))
    across, forwarded = [], []
    for n, (start, width) in enumerate(chunks):
        pair = jnp.stack([x[:, :, start : start + width] for x in (right, near)])
        before = across[-1:] + forwarded[-2:-1] if n else [landed]
        pair = after(pair, *before)
        across.append(along(pair, over_middle))
        if n + 1 < len(chunks):
            forwarded.append(along(across[-1], [(1, 0), (2, 3)]))
        else:
            forwarded.append(along(pair, [(2, 0), (1, 3)]))

    out, tile, waiting = None, None, []
    for n, (start, width) in enumerate(chunks):
        earlier = across[n + 1 : n + 2] * (n + 2 < len(chunks)) + ([] if tile is None else [tile])
        whole = pl.BlockSpec((2, 2, deep, width), lambda m: (0, 0, 0, 0))

        def columns_at(start):
            return pl.BlockSpec((2, deep, width), lambda m: (0, 0, start // width))

        tile = product(
            hi,
            lo,
            fill_shards,
            [
                after(table, *earlier),
                right,
                near,
                across[n],
                forwarded[n],
            ],
            [
                pl.BlockSpec(memory_space=pltpu.SMEM),
                columns_at(start),
                columns_at(start),
                whole,
                whole,
            ],
            count,
            width,
        )
        received = lax.all_to_all(tile, "col", split_axis=0, concat_axis=0, tiled=True)
        waiting.append(received)
        if n:
            out = place(waiting, out, start + width - sum(x.shape[3] for x in waiting), cols)
            waiting = []
    return out


def any_body(left, right, prefix_owner, qubit_order):
    row_count = lax.axis_size("row")
    col_count = lax.axis_size("col")
    _, rows, depth = left.shape
    _, deep, cols = right.shape
    width = cols // 4
    inverse = owner_inverse(prefix_owner)
    hot = qubit_one_hot(qubit_order)

    turned = jnp.transpose(left, (0, 2, 1)).reshape(row_count, 2 * depth // row_count, rows)
    spread = lax.all_to_all(turned, "row", split_axis=0, concat_axis=0, tiled=True)
    ordered = order_prefixes(spread, inverse)
    landed = lax.all_to_all(ordered, "row", split_axis=0, concat_axis=0, tiled=True)
    gathered = lax.all_gather(landed.reshape(2, depth, rows), "col", axis=0)
    hi, lo = prepare_left(gathered, hot)

    out = None
    for start in range(0, cols, width):
        piece = right[:, :, start : start + width]
        whole = lax.all_gather(piece, "row", axis=0)
        spec = pl.BlockSpec((row_count, 2, deep, width), lambda m: (0, 0, 0, 0))
        tile = product(hi, lo, fill_whole, [whole], [spec], col_count, width)
        received = lax.all_to_all(tile, "col", split_axis=0, concat_axis=0, tiled=True)
        out = place([received], out, start, cols)
    return out


def solution(mesh):
    in_specs = (P(None, "row", "col"), P(None, "row", "col"), P(), P())
    out_specs = P(None, ("row", "col"), None)
    line = mesh.shape["row"] == 4 and mesh.shape["col"] == 8
    body = line_body if line else any_body
    return jax.shard_map(body, mesh=mesh, in_specs=in_specs, out_specs=out_specs, check_vma=False)
```
